128 devices in a mesh: row: 8 (over y_lo, z), col: 16 (over y_hi, x, core).
Axes of the slice: x: 4, y: 4 (y_hi: 2, y_lo: 2; y = y_hi * 2 + y_lo), z: 4, core: 2. Of those that a mesh axis runs over, the one named last changes fastest.
Arguments:
- eigvecs: float32 [65536, 4096], P(('row', 'col')), may hold values from -6 to 6
- panels: float32 [3, 256, 65536], P(None, None, ('row', 'col')), may hold values from -0.09375 to 0.09375
- tri_factors: float32 [3, 256, 256], replicated, may hold values from -0.2 to 0.6, as said below
Outputs:
- back: float32 [65536, 4096], P('row', 'col')
The draws below stay inside these ranges and needn't reach their ends.
Inputs may be any that keep to these rules, and one draw needn't show every extreme that they name: `tri_factors`: each factor is upper triangular; diagonal entries lie in 0.2 to 0.6.
All inputs are finite; a program needn't handle non-finite values.
Results may differ from the reference program's by a relative error of at most 0.00013.
Values sent between devices are 32-bit elements; how exact they have to be, the bound alone decides.
No kernel may reach another device: no remote copies, remote signals or barrier semaphores. Data moves between devices by JAX's collectives and lax.ppermute only.
A program may use at most 128 MiB of HBM per device.

```python
import jax
import jax.numpy as jnp
from jax import lax

N = 65536
NB = 256
REFL = 3
K = 4096


def tri_factor(key):
    key_diag = jax.random.fold_in(key, 11)
    key_off = jax.random.fold_in(key, 23)
    diag_vals = jax.random.uniform(key_diag, (NB,), jnp.float32, 0.2, 0.6)
    off_vals = jnp.clip(0.03 * jax.random.normal(key_off, (NB, NB), jnp.float32), -0.2, 0.2)
    return jnp.triu(off_vals, 1) + jnp.diag(diag_vals)


def draw_tri_factors(key, part):
    return jnp.stack([tri_factor(jax.random.fold_in(key, 101 + 7 * index)) for index in range(REFL)], 0)


def shard_levels(rng, shape, cuts, smallest, top_value):
    loudness = 1.0
    for position, shards_of in cuts:
        steps = jax.random.uniform(jax.random.fold_in(jax.random.fold_in(rng, 6), position), (shards_of,), jnp.float32, smallest / len(cuts), top_value / len(cuts))
        loudness = loudness * jnp.repeat(jnp.exp(steps), shape[position] // shards_of).reshape((-1,) + (1,) * (len(shape) - 1 - position))
    return loudness


def normal_values(own_key, extent, scale, bound, cuts=(), dtype=jnp.bfloat16):
    entries = scale * jax.random.normal(own_key, extent, jnp.float32)
    if cuts:
        entries = entries * shard_levels(own_key, extent, cuts, -0.22, 0.18)
    return jnp.clip(entries, -bound, bound).astype(dtype)


def setup_inputs(seed: int = 0) -> dict:
    arg_keys = jax.random.split(jax.random.key(seed), 4)
    eigvecs = normal_values(arg_keys[0], (N, K), 1.0, 6.0, ((0, 128),), jnp.float32)
    panels = normal_values(arg_keys[1], (REFL, NB, N), (N // 16) ** -0.5, 0.09375, ((2, 128),), jnp.float32)
    tri_factors = draw_tri_factors(jax.random.fold_in(arg_keys[3], 71), 0)
    return {"eigvecs": eigvecs, "panels": panels, "tri_factors": tri_factors}


def product(left, right):
    return jnp.dot(left, right, precision=lax.Precision.HIGHEST, preferred_element_type=jnp.float32)


def spread(panel_t, right):
    return lax.dot_general(panel_t, right, (((0,), (0,)), ((), ())), precision=lax.Precision.HIGHEST, preferred_element_type=jnp.float32)


def shaped(raw, offset):
    count = raw.shape[0]
    width = raw.shape[1]
    place = lax.broadcasted_iota(jnp.int32, (count, width), 1)
    limit = offset + lax.broadcasted_iota(jnp.int32, (count, width), 0)
    return jnp.where(place < limit, jnp.float32(0.0), jnp.where(place == limit, jnp.float32(1.0), raw)).astype(jnp.float32)


def reference(eigvecs, panels, tri_factors):
    updated = eigvecs
    for index in reversed(range(REFL)):
        panel_t = shaped(panels[index], (index + 1) * NB)
        w_block = product(panel_t, updated)
        updated = updated - spread(panel_t, product(tri_factors[index], w_block))
    return updated
```

```python
import jax
import jax.numpy as jnp
from jax import lax
from jax.experimental import pallas as pl
from jax.experimental.pallas import tpu as pltpu
from jax.sharding import Mesh
from jax.sharding import PartitionSpec as P

AXES = ("ylo", "z", "yhi", "x", "core")
ROW = ("ylo", "z")
COL = ("yhi", "x", "core")


def exact(left, right):
    return jnp.dot(left, right, precision=lax.Precision.HIGHEST, preferred_element_type=jnp.float32)


def halves(values):
    high = values.astype(jnp.bfloat16)
    low = (values - high.astype(jnp.float32)).astype(jnp.bfloat16)
    return high, low


def triple(left, right, dims):
    left_high, left_low = halves(left)
    right_high, right_low = halves(right)

    def dot(a, b):
        return lax.dot_general(a, b, (dims, ((), ())), preferred_element_type=jnp.float32)

    return dot(left_high, right_high) + (dot(left_high, right_low) + dot(left_low, right_high))


def project_kernel(v_ref, e_ref, w_ref):
    @pl.when(pl.program_id(0) == 0)
    def _():
        w_ref[...] = jnp.zeros_like(w_ref)

    w_ref[...] += triple(v_ref[0], e_ref[...], ((1,), (0,)))


def project(vectors, block):
    pieces, count, depth = vectors.shape
    width = block.shape[1]
    return pl.pallas_call(
        project_kernel,
        grid=(pieces,),
        in_specs=[
            pl.BlockSpec((1, count, depth), lambda k: (k, 0, 0)),
            pl.BlockSpec((depth, width), lambda k: (k, 0)),
        ],
        out_specs=pl.BlockSpec((count, width), lambda k: (0, 0)),
        out_shape=jax.ShapeDtypeStruct((count, width), jnp.float32),
        compiler_params=pltpu.CompilerParams(vmem_limit_bytes=40 * 2**20),
        cost_estimate=pl.CostEstimate(
            flops=6 * pieces * count * depth * width,
            bytes_accessed=4 * pieces * depth * (count + width),
            transcendentals=0,
        ),
    )(vectors, block)


def update_kernel(v_ref, e_ref, y_ref, o_ref):
    o_ref[...] = e_ref[...] - triple(v_ref[0], y_ref[...], ((0,), (0,)))


def update(vectors, block, y):
    pieces, count, depth = vectors.shape
    width = block.shape[1]
    return pl.pallas_call(
        update_kernel,
        grid=(pieces,),
        in_specs=[
            pl.BlockSpec((1, count, depth), lambda k: (k, 0, 0)),
            pl.BlockSpec((depth, width), lambda k: (k, 0)),
            pl.BlockSpec((count, width), lambda k: (0, 0)),
        ],
        out_specs=pl.BlockSpec((depth, width), lambda k: (k, 0)),
        out_shape=jax.ShapeDtypeStruct(block.shape, jnp.float32),
        compiler_params=pltpu.CompilerParams(vmem_limit_bytes=40 * 2**20),
        cost_estimate=pl.CostEstimate(
            flops=6 * pieces * count * depth * width,
            bytes_accessed=4 * pieces * depth * (count + 2 * width),
            transcendentals=0,
        ),
    )(vectors, block, y)


def row_sum(values):
    groups = lax.axis_size(ROW)
    parts = lax.all_to_all(values, ROW, split_axis=0, concat_axis=0, tiled=True)
    total = jnp.sum(parts.reshape(groups, -1, parts.shape[1]), axis=0)
    spread = jnp.broadcast_to(total[None], (groups,) + total.shape).reshape(parts.shape)
    return lax.all_to_all(spread, ROW, split_axis=0, concat_axis=0, tiled=True)


def ring(size, step):
    return [(i, (i + step) % size) for i in range(size)]


def x_ring(held):
    size = lax.axis_size("x")
    result = list(held)
    lefts, rights = [], []
    for piece, start, where in held:
        y, x, core = where
        lefts.append((lax.ppermute(piece, "x", ring(size, 1)), start, (y, (x + size - 1) % size, core)))
        rights.append((lax.ppermute(piece, "x", ring(size, -1)), start, (y, (x + 1) % size, core)))
    for (left, start, where), (right, _, _) in zip(lefts, rights):
        y, x, core = where
        half = left.shape[0] // 2
        far = (y, (x + size - 1) % size, core)
        result.append((lax.ppermute(left[:half], "x", ring(size, 1)), start, far))
        result.append((lax.ppermute(right[half:], "x", ring(size, -1)), start + half, far))
    return result + lefts + rights


def pair(held, axis, place):
    result = list(held)
    for piece, start, where in held:
        there = list(where)
        there[place] = 1 - there[place]
        result.append((lax.ppermute(piece, axis, ring(2, 1)), start, tuple(there)))
    return result


def gather(panels):
    count, depth = panels.shape
    cut = 2 * count // 3
    here = (lax.axis_index("yhi"), lax.axis_index("x"), lax.axis_index("core"))
    first = [(panels[cut:], cut, here)]
    second = [(panels[:cut], 0, here)]
    second = x_ring(pair(second, "yhi", 0))
    first = pair(x_ring(first), "yhi", 0)
    held = pair(first + second, "core", 2)
    sizes = (2, lax.axis_size("x"), 2)
    full = jnp.zeros((sizes[0] * sizes[1] * sizes[2], count, depth), jnp.float32)
    for piece, start, (y, x, core) in held:
        place = (y * sizes[1] + x) * sizes[2] + core
        full = lax.dynamic_update_slice(full, piece[None], (place, start, 0))
    return full


def on_device(eigvecs, panels, tri_factors):
    count, block_size, depth = panels.shape
    total = count * block_size
    row = lax.axis_index(ROW)
    col = lax.axis_index(COL)
    place = (row * lax.axis_size(COL) + col) * depth + lax.broadcasted_iota(jnp.int32, (total, depth), 1)
    limit = block_size + lax.broadcasted_iota(jnp.int32, (total, depth), 0)
    shaped = panels.reshape(total, depth)
    shaped = jnp.where(place < limit, 0.0, jnp.where(place == limit, 1.0, shaped))
    block = lax.all_to_all(eigvecs, COL, split_axis=1, concat_axis=0, tiled=True)
    vectors = gather(shaped)
    gram = lax.psum(jnp.concatenate([
        lax.dot_general(
            shaped[:block_size],
            shaped[block_size:],
            (((1,), (1,)), ((), ())),
            precision=lax.Precision.HIGHEST,
            preferred_element_type=jnp.float32,
        ),
        lax.dot_general(
            shaped[block_size : 2 * block_size],
            shaped[2 * block_size :],
            (((1,), (1,)), ((), ())),
            precision=lax.Precision.HIGHEST,
            preferred_element_type=jnp.float32,
        ),
    ], axis=1), AXES)
    g01, g02, g12 = (gram[:, i * block_size : (i + 1) * block_size] for i in range(3))
    t0, t1, t2 = (tri_factors[i] for i in range(3))
    m12 = -exact(t1, exact(g12, t2))
    m01 = -exact(t0, exact(g01, t1))
    m02 = -exact(t0, exact(g02, t2) + exact(g01, m12))
    zero = jnp.zeros_like(t0)
    mixer = jnp.concatenate([
        jnp.concatenate([t0, m01, m02], axis=1),
        jnp.concatenate([zero, t1, m12], axis=1),
        jnp.concatenate([zero, zero, t2], axis=1),
    ], axis=0)
    w = row_sum(project(vectors, block))
    return update(vectors, block, exact(mixer, w))


def solution(mesh):
    fine = Mesh(mesh.devices.reshape(2, 4, 2, 4, 2), AXES)
    in_specs = (P(AXES, None), P(None, None, AXES), P())
    out_specs = P(ROW, COL)
    return jax.shard_map(on_device, mesh=fine, in_specs=in_specs, out_specs=out_specs, check_vma=False)
```

```python
import functools

import jax
import jax.numpy as jnp
from jax import lax
from jax.experimental import pallas as pl
from jax.experimental.pallas import tpu as pltpu
from jax.sharding import Mesh
from jax.sharding import PartitionSpec as P

AXES = ("ylo", "z", "yhi", "x", "core")
ROW = ("ylo", "z")
COL = ("yhi", "x", "core")


def halves(values):
    high = values.astype(jnp.bfloat16)
    low = (values - high.astype(jnp.float32)).astype(jnp.bfloat16)
    return high, low


def triple(left, right, dims):
    left_high, left_low = halves(left)
    right_high, right_low = halves(right)

    def dot(a, b):
        return lax.dot_general(a, b, (dims, ((), ())), preferred_element_type=jnp.float32)

    return dot(left_high, right_high) + (dot(left_high, right_low) + dot(left_low, right_high))


def fetch(sources, places, k, buffers, sems):
    slot = lax.rem(k, 2)
    for n, (source, buffer) in enumerate(zip(sources, buffers)):
        sem = sems.at[n, slot]
        if isinstance(source, list):
            for i, piece in enumerate(source):

                @pl.when(k == i)
                def _(piece=piece):
                    pltpu.make_async_copy(piece, buffer.at[slot], sem).start()

        else:
            depth = buffer.shape[1]
            rows = pl.ds(pl.multiple_of(places[k] * depth, depth), depth)
            pltpu.make_async_copy(source.at[rows], buffer.at[slot], sem).start()


def arrive(k, buffers, sems):
    slot = lax.rem(k, 2)
    for n, buffer in enumerate(buffers):
        pltpu.make_async_copy(buffer.at[slot], buffer.at[slot], sems.at[n, slot]).wait()
    return slot


def pass_kernel(blocks, has_old, has_new, places, e_ref, *rest):
    rest = list(rest)
    old = [rest.pop(0) for _ in range(blocks)] if has_old else None
    new = [rest.pop(0) for _ in range(blocks)] if has_new else None
    if has_old:
        t_ref, sum_ref = rest.pop(0), rest.pop(0)
        o_ref = rest.pop(0)
    if has_new:
        w_ref = rest.pop(0)
    sources, buffers = [e_ref], [rest.pop(0)]
    if has_old:
        sources.append(old)
        buffers.append(rest.pop(0))
    if has_new:
        sources.append(new)
        buffers.append(rest.pop(0))
    if has_old:
        o_buf, y_ref, o_sems = rest.pop(0), rest.pop(0), rest.pop(0)
    sems = rest.pop(0)
    depth = buffers[0].shape[1]

    def leave(k):
        slot = lax.rem(k, 2)
        rows = pl.ds(pl.multiple_of(places[k] * depth, depth), depth)
        return pltpu.make_async_copy(o_buf.at[slot], o_ref.at[rows], o_sems.at[slot])

    fetch(sources, places, 0, buffers, sems)
    if has_old:
        y_ref[...] = triple(t_ref[...], sum_ref[...], ((1,), (0,)))
    if has_new:
        w_ref[...] = jnp.zeros_like(w_ref)

    @pl.loop(0, blocks)
    def _(k):
        @pl.when(k + 1 < blocks)
        def _():
            fetch(sources, places, k + 1, buffers, sems)

        slot = arrive(k, buffers, sems)
        block = buffers[0][slot]
        if has_old:

            @pl.when(k >= 2)
            def _():
                leave(k - 2).wait()

            block = block - triple(buffers[1][slot], y_ref[...], ((0,), (0,)))
            o_buf[slot] = block
            leave(k).start()
        if has_new:
            w_ref[...] += triple(buffers[-1][slot], block, ((1,), (0,)))

    if has_old:
        leave(blocks - 2).wait()
        leave(blocks - 1).wait()


def one_pass(places, block, old=None, factor=None, total=None, new=None):
    pieces = old if old is not None else new
    blocks = len(pieces)
    count, depth = pieces[0].shape
    width = block.shape[1]
    far = pl.BlockSpec(memory_space=pltpu.HBM)
    near = pl.BlockSpec(memory_space=pltpu.VMEM)
    operands, in_specs = [places, block], [pl.BlockSpec(memory_space=pltpu.SMEM), far]
    out_specs, out_shape = [], []
    scratch = [pltpu.VMEM((2, depth, width), jnp.float32)]
    products = 0
    for pieces in (old, new):
        if pieces is not None:
            operands += pieces
            in_specs += [far] * blocks
            scratch.append(pltpu.VMEM((2, count, depth), jnp.float32))
            products += 1
    if old is not None:
        operands += [factor, total]
        in_specs += [near, near]
        out_specs.append(far)
        out_shape.append(jax.ShapeDtypeStruct(block.shape, jnp.float32))
        scratch += [
            pltpu.VMEM((2, depth, width), jnp.float32),
            pltpu.VMEM((count, width), jnp.float32),
            pltpu.SemaphoreType.DMA((2,)),
        ]
    if new is not None:
        out_specs.append(near)
        out_shape.append(jax.ShapeDtypeStruct((count, width), jnp.float32))
    scratch.append(pltpu.SemaphoreType.DMA((1 + products, 2)))
    return pl.pallas_call(
        functools.partial(pass_kernel, blocks, old is not None, new is not None),
        in_specs=in_specs,
        out_specs=out_specs,
        out_shape=out_shape,
        scratch_shapes=scratch,
        compiler_params=pltpu.CompilerParams(vmem_limit_bytes=60 * 2**20),
        cost_estimate=pl.CostEstimate(
            flops=6 * products * blocks * count * depth * width,
            bytes_accessed=4 * blocks * depth * (products * count + 2 * width),
            transcendentals=0,
        ),
    )(*operands)


def exchange_sum(values, axes):
    groups = lax.axis_size(axes)
    parts = lax.all_to_all(values, axes, split_axis=0, concat_axis=0, tiled=True)
    total = jnp.sum(parts.reshape(groups, -1, parts.shape[1]), axis=0)
    spread = jnp.broadcast_to(total[None], (groups,) + total.shape).reshape(parts.shape)
    return lax.all_to_all(spread, axes, split_axis=0, concat_axis=0, tiled=True)


def turn(sign):
    size = lax.axis_size("x")
    pairs = []
    for x in range(size):
        for core in range(2):
            step = sign if core == 0 else -sign
            pairs.append((x * 2 + core, (x + step) % size * 2 + core))
    return pairs


def x_ring(piece):
    near = lax.ppermute(piece, ("x", "core"), turn(1))
    other = lax.ppermute(piece, ("x", "core"), turn(-1))
    far = lax.ppermute(near, ("x", "core"), turn(1))
    return [piece, near, other, far]


def swap(piece, axis):
    return lax.ppermute(piece, axis, [(0, 1), (1, 0)])


def gather(piece, x_first):
    if x_first:
        held = x_ring(piece)
        held = held + [swap(part, "yhi") for part in held]
    else:
        held = x_ring(piece) + x_ring(swap(piece, "yhi"))
    return held + [swap(part, "core") for part in held]


def block_places():
    size = lax.axis_size("x")
    yhi, x, core = (lax.axis_index(name) for name in COL)
    places = []
    for c in (core, 1 - core):
        sign = 1 - 2 * c
        for y in (yhi, 1 - yhi):
            for step in (0, -1, 1, -2):
                places.append((y * size + lax.rem(x + sign * step + size, size)) * 2 + c)
    return jnp.stack(places).astype(jnp.int32)


def on_device(eigvecs, panels, tri_factors):
    count, block_size, depth = panels.shape
    start = (lax.axis_index(ROW) * lax.axis_size(COL) + lax.axis_index(COL)) * depth
    place = start + lax.broadcasted_iota(jnp.int32, (block_size, depth), 1)
    limit = lax.broadcasted_iota(jnp.int32, (block_size, depth), 0)
    vectors = []
    for j in reversed(range(count)):
        gap = place - limit - (j + 1) * block_size
        shaped = jnp.where(gap < 0, 0.0, jnp.where(gap == 0, 1.0, panels[j]))
        vectors.append(gather(shaped, j % 2 == 1))
    places = block_places()
    block = lax.all_to_all(eigvecs, COL, split_axis=1, concat_axis=0, tiled=True)
    (w,) = one_pass(places, block, new=vectors[0])
    for i in range(count):
        factor = tri_factors[count - 1 - i]
        total = exchange_sum(w, ROW)
        if i + 1 < count:
            block, w = one_pass(places, block, vectors[i], factor, total, vectors[i + 1])
        else:
            (block,) = one_pass(places, block, vectors[i], factor, total)
    return block


def solution(mesh):
    fine = Mesh(mesh.devices.reshape(2, 4, 2, 4, 2), AXES)
    in_specs = (P(AXES, None), P(None, None, AXES), P())
    out_specs = P(ROW, COL)
    return jax.shard_map(on_device, mesh=fine, in_specs=in_specs, out_specs=out_specs, check_vma=False)
```

```python
import functools

import jax
import jax.numpy as jnp
from jax import lax
from jax.experimental import pallas as pl
from jax.experimental.pallas import tpu as pltpu
from jax.sharding import Mesh
from jax.sharding import PartitionSpec as P

AXES = ("ylo", "z", "yhi", "x", "core")
ROW = ("ylo", "z")
COL = ("yhi", "x", "core")


def halves(values):
    high = values.astype(jnp.bfloat16)
    low = (values - high.astype(jnp.float32)).astype(jnp.bfloat16)
    return high, low


def triple(left, right, dims):
    left_high, left_low = halves(left)
    right_high, right_low = halves(right)

    def dot(a, b):
        return lax.dot_general(a, b, (dims, ((), ())), preferred_element_type=jnp.float32)

    return dot(left_high, right_high) + (dot(left_high, right_low) + dot(left_low, right_high))


LIMIT = pltpu.CompilerParams(vmem_limit_bytes=60 * 2**20)


def fetch(parts, buffer, sem):
    start = 0
    for part in parts:
        rows = part.shape[0]
        pltpu.make_async_copy(part, buffer.at[pl.ds(start, rows)], sem).start()
        start += rows


def arrive(buffer, sem):
    pltpu.make_async_copy(buffer, buffer, sem).wait()


def block_rows(ref, places, k, depth):
    return ref.at[pl.ds(pl.multiple_of(places[k] * depth, depth), depth)]


def grouped(flat, blocks):
    size = len(flat) // blocks
    return [flat[k * size : (k + 1) * size] for k in range(blocks)]


def gram_kernel(blocks, size, *refs):
    flat, (g_ref, v_buf, v_sems) = refs[:-3], refs[-3:]
    for k, parts in enumerate(grouped(flat, blocks)):
        fetch(parts, v_buf.at[k], v_sems.at[k])
    g_ref[...] = jnp.zeros_like(g_ref)

    @pl.loop(0, blocks)
    def _(k):
        arrive(v_buf.at[k], v_sems.at[k])
        first, second, third = (v_buf[k, pl.ds(j * size, size)] for j in range(3))
        across = ((1,), (1,))
        g_ref[0] += triple(first, second, across)
        g_ref[1] += triple(first, third, across)
        g_ref[2] += triple(second, third, across)


def project_kernel(blocks, places, e_ref, *refs):
    flat, (w_ref, e_buf, v_buf, e_sems, v_sems) = refs[:-5], refs[-5:]
    depth = e_buf.shape[1]
    for k, parts in enumerate(grouped(flat, blocks)):
        pltpu.make_async_copy(block_rows(e_ref, places, k, depth), e_buf.at[k], e_sems.at[k]).start()
        fetch(parts, v_buf.at[k], v_sems.at[k])
    w_ref[...] = jnp.zeros_like(w_ref)

    @pl.loop(0, blocks)
    def _(k):
        arrive(e_buf.at[k], e_sems.at[k])
        arrive(v_buf.at[k], v_sems.at[k])
        w_ref[...] += triple(v_buf[k], e_buf[k], ((1,), (0,)))


def apply_kernel(blocks, places, e_ref, m_ref, w_ref, *refs):
    flat, (o_ref, e_buf, v_buf, y_ref, e_sems, v_sems, o_sems) = refs[:-7], refs[-7:]
    depth = e_buf.shape[1]
    for k, parts in enumerate(grouped(flat, blocks)):
        pltpu.make_async_copy(block_rows(e_ref, places, k, depth), e_buf.at[k], e_sems.at[k]).start()
        fetch(parts, v_buf.at[k], v_sems.at[k])
    y_ref[...] = triple(m_ref[...], w_ref[...], ((1,), (0,)))

    def leave(k):
        return pltpu.make_async_copy(e_buf.at[k], block_rows(o_ref, places, k, depth), o_sems.at[k])

    @pl.loop(0, blocks)
    def _(k):
        arrive(e_buf.at[k], e_sems.at[k])
        arrive(v_buf.at[k], v_sems.at[k])
        e_buf[k] = e_buf[k] - triple(v_buf[k], y_ref[...], ((0,), (0,)))
        leave(k).start()

    @pl.loop(0, blocks)
    def _(k):
        leave(k).wait()


FAR = pl.BlockSpec(memory_space=pltpu.HBM)
NEAR = pl.BlockSpec(memory_space=pltpu.VMEM)
SCALARS = pl.BlockSpec(memory_space=pltpu.SMEM)


def cost(blocks, count, depth, width, passes):
    return pl.CostEstimate(
        flops=6 * blocks * count * depth * width,
        bytes_accessed=4 * blocks * depth * (count + passes * width),
        transcendentals=0,
    )


def sizes_of(pieces):
    return len(pieces), sum(part.shape[0] for part in pieces[0]), pieces[0][0].shape[1]


def gram_of(pieces, size):
    blocks, count, depth = sizes_of(pieces)
    flat = [part for parts in pieces for part in parts]
    return pl.pallas_call(
        functools.partial(gram_kernel, blocks, size),
        in_specs=[FAR] * len(flat),
        out_specs=NEAR,
        out_shape=jax.ShapeDtypeStruct((3, size, size), jnp.float32),
        scratch_shapes=[pltpu.VMEM((blocks, count, depth), jnp.float32), pltpu.SemaphoreType.DMA((blocks,))],
        compiler_params=LIMIT,
        cost_estimate=cost(blocks, count, depth, size, 0),
    )(*flat)


def project(places, block, pieces):
    blocks, count, depth = sizes_of(pieces)
    width = block.shape[1]
    flat = [part for parts in pieces for part in parts]
    return pl.pallas_call(
        functools.partial(project_kernel, blocks),
        in_specs=[SCALARS, FAR] + [FAR] * len(flat),
        out_specs=NEAR,
        out_shape=jax.ShapeDtypeStruct((count, width), jnp.float32),
        scratch_shapes=[
            pltpu.VMEM((blocks, depth, width), jnp.float32),
            pltpu.VMEM((blocks, count, depth), jnp.float32),
            pltpu.SemaphoreType.DMA((blocks,)),
            pltpu.SemaphoreType.DMA((blocks,)),
        ],
        compiler_params=LIMIT,
        cost_estimate=cost(blocks, count, depth, width, 1),
    )(places, block, *flat)


def apply(places, block, mixer, w, pieces):
    blocks, count, depth = sizes_of(pieces)
    width = block.shape[1]
    flat = [part for parts in pieces for part in parts]
    return pl.pallas_call(
        functools.partial(apply_kernel, blocks),
        in_specs=[SCALARS, FAR, NEAR, NEAR] + [FAR] * len(flat),
        out_specs=FAR,
        out_shape=jax.ShapeDtypeStruct(block.shape, jnp.float32),
        scratch_shapes=[
            pltpu.VMEM((blocks, depth, width), jnp.float32),
            pltpu.VMEM((blocks, count, depth), jnp.float32),
            pltpu.VMEM((count, width), jnp.float32),
            pltpu.SemaphoreType.DMA((blocks,)),
            pltpu.SemaphoreType.DMA((blocks,)),
            pltpu.SemaphoreType.DMA((blocks,)),
        ],
        compiler_params=LIMIT,
        cost_estimate=cost(blocks, count, depth, width, 2),
    )(places, block, mixer, w, *flat)


def mix_kernel(t_ref, g_ref, m_ref):
    size = t_ref.shape[1]

    def times(left, right):
        return triple(left, right, ((1,), (0,)))

    m_ref[...] = jnp.zeros_like(m_ref)
    for j in range(3):
        m_ref[pl.ds(j * size, size), pl.ds(j * size, size)] = t_ref[j]
    middle = -times(t_ref[1], times(g_ref[2], t_ref[2]))
    m_ref[pl.ds(size, size), pl.ds(2 * size, size)] = middle
    m_ref[pl.ds(0, size), pl.ds(size, size)] = -times(t_ref[0], times(g_ref[0], t_ref[1]))
    far = times(g_ref[1], t_ref[2]) + times(g_ref[0], middle)
    m_ref[pl.ds(0, size), pl.ds(2 * size, size)] = -times(t_ref[0], far)


def mix(tri_factors, gram):
    size = 3 * tri_factors.shape[1]
    return pl.pallas_call(
        mix_kernel,
        in_specs=[NEAR, NEAR],
        out_specs=NEAR,
        out_shape=jax.ShapeDtypeStruct((size, size), jnp.float32),
        compiler_params=LIMIT,
    )(tri_factors, gram)


def columns_kernel(e_ref, o_ref, buf, in_sems, out_sems):
    blocks, depth, width = buf.shape
    arrivals = [
        pltpu.make_async_copy(e_ref.at[:, pl.ds(k * width, width)], buf.at[k], in_sems.at[k]) for k in range(blocks)
    ]
    leaves = [
        pltpu.make_async_copy(buf.at[k], o_ref.at[pl.ds(k * depth, depth)], out_sems.at[k]) for k in range(blocks)
    ]
    for copy in arrivals:
        copy.start()
    for arrival, leave in zip(arrivals, leaves):
        arrival.wait()
        leave.start()
    for leave in leaves:
        leave.wait()


def columns_apart(eigvecs, blocks):
    depth, width = eigvecs.shape[0], eigvecs.shape[1] // blocks
    return pl.pallas_call(
        columns_kernel,
        in_specs=[pl.BlockSpec(memory_space=pltpu.HBM)],
        out_specs=pl.BlockSpec(memory_space=pltpu.HBM),
        out_shape=jax.ShapeDtypeStruct((blocks * depth, width), jnp.float32),
        scratch_shapes=[
            pltpu.VMEM((blocks, depth, width), jnp.float32),
            pltpu.SemaphoreType.DMA((blocks,)),
            pltpu.SemaphoreType.DMA((blocks,)),
        ],
        compiler_params=LIMIT,
        cost_estimate=pl.CostEstimate(flops=0, bytes_accessed=8 * blocks * depth * width, transcendentals=0),
    )(eigvecs)


def scattered(values, axes):
    return lax.all_to_all(values, axes, split_axis=0, concat_axis=0, tiled=True)


def collected(parts, axes):
    groups = lax.axis_size(axes)
    total = jnp.sum(parts.reshape(groups, -1, parts.shape[1]), axis=0)
    spread = jnp.broadcast_to(total[None], (groups,) + total.shape).reshape(parts.shape)
    return lax.all_to_all(spread, axes, split_axis=0, concat_axis=0, tiled=True)


def turn(sign):
    size = lax.axis_size("x")
    pairs = []
    for x in range(size):
        for core in range(2):
            step = sign if core == 0 else -sign
            pairs.append((x * 2 + core, (x + step) % size * 2 + core))
    return pairs


def send(piece, sign):
    return lax.ppermute(piece, ("x", "core"), turn(sign))


def swap(piece, axis):
    return lax.ppermute(piece, axis, [(0, 1), (1, 0)])


def block_places():
    size = lax.axis_size("x")
    yhi, x, core = (lax.axis_index(name) for name in COL)
    places = []
    for c in (core, 1 - core):
        sign = 1 - 2 * c
        for y in (yhi, 1 - yhi):
            for step in (0, -1, 1, -2):
                places.append((y * size + lax.rem(x + sign * step + size, size)) * 2 + c)
    return jnp.stack(places).astype(jnp.int32)


def after(values, *done):
    tied = lax.optimization_barrier((*values, *done))
    return tied[: len(values)], tied[len(values) :]


def on_device(eigvecs, panels, tri_factors):
    count, block_size, depth = panels.shape
    start = (lax.axis_index(ROW) * lax.axis_size(COL) + lax.axis_index(COL)) * depth
    place = start + lax.broadcasted_iota(jnp.int32, (block_size, depth), 1)
    limit = lax.broadcasted_iota(jnp.int32, (block_size, depth), 0)
    shaped = []
    for j in range(count):
        gap = place - limit - (j + 1) * block_size
        shaped.append(jnp.where(gap < 0, 0.0, jnp.where(gap == 0, 1.0, panels[j])))
    places = block_places()
    block = columns_apart(eigvecs, lax.axis_size(COL))

    wide = jnp.concatenate(shaped[:2], axis=0)
    slim = shaped[2]
    wide_there = swap(wide, "yhi")
    slim_near, slim_other = send(slim, 1), send(slim, -1)
    wide_near, wide_other = send(wide, 1), send(wide, -1)
    slim_held = [slim, slim_near, slim_other, send(slim_near, 1)]
    wide_far = send(wide_near, 1)
    wide_held = [wide, wide_near, wide_other, wide_far, wide_there, send(wide_there, 1), send(wide_there, -1)]
    slim_held += [swap(part, "yhi") for part in slim_held]
    wide_held += [send(wide_held[5], 1)]
    (block,), held = after((block,), *wide_held[1:], *slim_held[1:])
    wide_held[1:], slim_held[1:] = held[:7], held[7:]
    block = lax.all_to_all(block, COL, split_axis=0, concat_axis=0, tiled=True)
    pieces = list(zip(wide_held, slim_held))
    pieces += [tuple(swap(part, "core") for part in parts) for parts in pieces]

    gram = gram_of(pieces, block_size)
    size = lax.axis_size("z")
    for step in (1, 2):
        gram = gram + lax.ppermute(gram, "z", [(i, i ^ step) for i in range(size)])
    (gram,), (block,) = after((gram,), block)
    gram = gram + swap(gram, "ylo")
    mixer = mix(tri_factors, gram)
    w = collected(scattered(project(places, block, pieces), ROW), ROW)
    return apply(places, block, mixer, w, pieces)


def solution(mesh):
    fine = Mesh(mesh.devices.reshape(2, 4, 2, 4, 2), AXES)
    in_specs = (P(AXES, None), P(None, None, AXES), P())
    out_specs = P(ROW, COL)
    return jax.shard_map(on_device, mesh=fine, in_specs=in_specs, out_specs=out_specs, check_vma=False)
```

```python
import functools

import jax
import jax.numpy as jnp
from jax import lax
from jax.experimental import pallas as pl
from jax.experimental.pallas import tpu as pltpu
from jax.sharding import Mesh
from jax.sharding import PartitionSpec as P

AXES = ("ylo", "z", "yhi", "x", "core")
ROW = ("ylo", "z")
COL = ("yhi", "x", "core")


def halves(values):
    high = values.astype(jnp.bfloat16)
    low = (values - high.astype(jnp.float32)).astype(jnp.bfloat16)
    return high, low


def triple(left, right, dims):
    left_high, left_low = halves(left)
    right_high, right_low = halves(right)

    def dot(a, b):
        return lax.dot_general(a, b, (dims, ((), ())), preferred_element_type=jnp.float32)

    return dot(left_high, right_high) + (dot(left_high, right_low) + dot(left_low, right_high))


AHEAD = 3
LIMIT = pltpu.CompilerParams(vmem_limit_bytes=60 * 2**20)


def fetch(parts, buffer, sem):
    start = 0
    for part in parts:
        rows = part.shape[0]
        pltpu.make_async_copy(part, buffer.at[pl.ds(start, rows)], sem).start()
        start += rows


def arrive(buffer, sem):
    pltpu.make_async_copy(buffer, buffer, sem).wait()


def block_rows(ref, places, k, depth):
    return ref.at[pl.ds(pl.multiple_of(places[k] * depth, depth), depth)]


def grouped(flat, blocks):
    size = len(flat) // blocks
    return [flat[k * size : (k + 1) * size] for k in range(blocks)]


def fetch_block(pieces, places, k, e_ref, e_buf, e_sems, v_buf, v_sems):
    pltpu.make_async_copy(block_rows(e_ref, places, k, e_buf.shape[1]), e_buf.at[k], e_sems.at[k]).start()
    fetch_pieces(pieces, k, v_buf, v_sems)


def fetch_pieces(pieces, k, v_buf, v_sems):
    for i, parts in enumerate(pieces):
        if isinstance(k, int):
            if k == i:
                fetch(parts, v_buf.at[i], v_sems.at[i])
        else:

            @pl.when(k == i)
            def _(parts=parts, i=i):
                fetch(parts, v_buf.at[i], v_sems.at[i])


def gram_kernel(blocks, size, *refs):
    flat, (g_ref, v_buf, v_sems) = refs[:-3], refs[-3:]
    pieces = grouped(flat, blocks)
    for k in range(AHEAD):
        fetch_pieces(pieces, k, v_buf, v_sems)
    g_ref[...] = jnp.zeros_like(g_ref)

    @pl.loop(0, blocks)
    def _(k):
        @pl.when(k + AHEAD < blocks)
        def _():
            fetch_pieces(pieces, k + AHEAD, v_buf, v_sems)

        arrive(v_buf.at[k], v_sems.at[k])
        first, second, third = (v_buf[k, pl.ds(j * size, size)] for j in range(3))
        across = ((1,), (1,))
        g_ref[0] += triple(first, second, across)
        g_ref[1] += triple(first, third, across)
        g_ref[2] += triple(second, third, across)


def project_kernel(blocks, places, e_ref, *refs):
    flat, (w_ref, e_buf, v_buf, e_sems, v_sems) = refs[:-5], refs[-5:]
    pieces = grouped(flat, blocks)
    for k in range(AHEAD):
        fetch_block(pieces, places, k, e_ref, e_buf, e_sems, v_buf, v_sems)
    w_ref[...] = jnp.zeros_like(w_ref)

    @pl.loop(0, blocks)
    def _(k):
        @pl.when(k + AHEAD < blocks)
        def _():
            fetch_block(pieces, places, k + AHEAD, e_ref, e_buf, e_sems, v_buf, v_sems)

        arrive(e_buf.at[k], e_sems.at[k])
        arrive(v_buf.at[k], v_sems.at[k])
        w_ref[...] += triple(v_buf[k], e_buf[k], ((1,), (0,)))


def apply_kernel(blocks, places, e_ref, m_ref, w_ref, *refs):
    flat, (o_ref, e_buf, v_buf, y_ref, e_sems, v_sems, o_sems) = refs[:-7], refs[-7:]
    depth = e_buf.shape[1]
    pieces = grouped(flat, blocks)
    for k in range(AHEAD):
        fetch_block(pieces, places, k, e_ref, e_buf, e_sems, v_buf, v_sems)
    y_ref[...] = triple(m_ref[...], w_ref[...], ((1,), (0,)))

    def leave(k):
        return pltpu.make_async_copy(e_buf.at[k], block_rows(o_ref, places, k, depth), o_sems.at[k])

    @pl.loop(0, blocks)
    def _(k):
        @pl.when(k + AHEAD < blocks)
        def _():
            fetch_block(pieces, places, k + AHEAD, e_ref, e_buf, e_sems, v_buf, v_sems)

        arrive(e_buf.at[k], e_sems.at[k])
        arrive(v_buf.at[k], v_sems.at[k])
        e_buf[k] = e_buf[k] - triple(v_buf[k], y_ref[...], ((0,), (0,)))
        leave(k).start()

    @pl.loop(0, blocks)
    def _(k):
        leave(k).wait()


FAR = pl.BlockSpec(memory_space=pltpu.HBM)
NEAR = pl.BlockSpec(memory_space=pltpu.VMEM)
SCALARS = pl.BlockSpec(memory_space=pltpu.SMEM)


def cost(blocks, count, depth, width, passes):
    return pl.CostEstimate(
        flops=6 * blocks * count * depth * width,
        bytes_accessed=4 * blocks * depth * (count + passes * width),
        transcendentals=0,
    )


def sizes_of(pieces):
    return len(pieces), sum(part.shape[0] for part in pieces[0]), pieces[0][0].shape[1]


def gram_of(pieces, size):
    blocks, count, depth = sizes_of(pieces)
    flat = [part for parts in pieces for part in parts]
    return pl.pallas_call(
        functools.partial(gram_kernel, blocks, size),
        in_specs=[FAR] * len(flat),
        out_specs=NEAR,
        out_shape=jax.ShapeDtypeStruct((3, size, size), jnp.float32),
        scratch_shapes=[pltpu.VMEM((blocks, count, depth), jnp.float32), pltpu.SemaphoreType.DMA((blocks,))],
        compiler_params=LIMIT,
        cost_estimate=cost(blocks, count, depth, size, 0),
    )(*flat)


def project(places, block, pieces):
    blocks, count, depth = sizes_of(pieces)
    width = block.shape[1]
    flat = [part for parts in pieces for part in parts]
    return pl.pallas_call(
        functools.partial(project_kernel, blocks),
        in_specs=[SCALARS, FAR] + [FAR] * len(flat),
        out_specs=NEAR,
        out_shape=jax.ShapeDtypeStruct((count, width), jnp.float32),
        scratch_shapes=[
            pltpu.VMEM((blocks, depth, width), jnp.float32),
            pltpu.VMEM((blocks, count, depth), jnp.float32),
            pltpu.SemaphoreType.DMA((blocks,)),
            pltpu.SemaphoreType.DMA((blocks,)),
        ],
        compiler_params=LIMIT,
        cost_estimate=cost(blocks, count, depth, width, 1),
    )(places, block, *flat)


def apply(places, block, mixer, w, pieces):
    blocks, count, depth = sizes_of(pieces)
    width = block.shape[1]
    flat = [part for parts in pieces for part in parts]
    return pl.pallas_call(
        functools.partial(apply_kernel, blocks),
        in_specs=[SCALARS, FAR, NEAR, NEAR] + [FAR] * len(flat),
        out_specs=FAR,
        out_shape=jax.ShapeDtypeStruct(block.shape, jnp.float32),
        scratch_shapes=[
            pltpu.VMEM((blocks, depth, width), jnp.float32),
            pltpu.VMEM((blocks, count, depth), jnp.float32),
            pltpu.VMEM((count, width), jnp.float32),
            pltpu.SemaphoreType.DMA((blocks,)),
            pltpu.SemaphoreType.DMA((blocks,)),
            pltpu.SemaphoreType.DMA((blocks,)),
        ],
        compiler_params=LIMIT,
        cost_estimate=cost(blocks, count, depth, width, 2),
    )(places, block, mixer, w, *flat)


def mix_kernel(t_ref, g_ref, m_ref):
    size = t_ref.shape[1]

    def times(left, right):
        return triple(left, right, ((1,), (0,)))

    m_ref[...] = jnp.zeros_like(m_ref)
    for j in range(3):
        m_ref[pl.ds(j * size, size), pl.ds(j * size, size)] = t_ref[j]
    middle = -times(t_ref[1], times(g_ref[2], t_ref[2]))
    m_ref[pl.ds(size, size), pl.ds(2 * size, size)] = middle
    m_ref[pl.ds(0, size), pl.ds(size, size)] = -times(t_ref[0], times(g_ref[0], t_ref[1]))
    far = times(g_ref[1], t_ref[2]) + times(g_ref[0], middle)
    m_ref[pl.ds(0, size), pl.ds(2 * size, size)] = -times(t_ref[0], far)


def mix(tri_factors, gram):
    size = 3 * tri_factors.shape[1]
    return pl.pallas_call(
        mix_kernel,
        in_specs=[NEAR, NEAR],
        out_specs=NEAR,
        out_shape=jax.ShapeDtypeStruct((size, size), jnp.float32),
        compiler_params=LIMIT,
    )(tri_factors, gram)


def columns_kernel(e_ref, o_ref, buf, in_sems, out_sems):
    blocks, depth, width = buf.shape
    arrivals = [
        pltpu.make_async_copy(e_ref.at[:, pl.ds(k * width, width)], buf.at[k], in_sems.at[k]) for k in range(blocks)
    ]
    leaves = [
        pltpu.make_async_copy(buf.at[k], o_ref.at[pl.ds(k * depth, depth)], out_sems.at[k]) for k in range(blocks)
    ]
    for copy in arrivals:
        copy.start()
    for arrival, leave in zip(arrivals, leaves):
        arrival.wait()
        leave.start()
    for leave in leaves:
        leave.wait()


def columns_apart(eigvecs, blocks):
    depth, width = eigvecs.shape[0], eigvecs.shape[1] // blocks
    return pl.pallas_call(
        columns_kernel,
        in_specs=[pl.BlockSpec(memory_space=pltpu.HBM)],
        out_specs=pl.BlockSpec(memory_space=pltpu.HBM),
        out_shape=jax.ShapeDtypeStruct((blocks * depth, width), jnp.float32),
        scratch_shapes=[
            pltpu.VMEM((blocks, depth, width), jnp.float32),
            pltpu.SemaphoreType.DMA((blocks,)),
            pltpu.SemaphoreType.DMA((blocks,)),
        ],
        compiler_params=LIMIT,
        cost_estimate=pl.CostEstimate(flops=0, bytes_accessed=8 * blocks * depth * width, transcendentals=0),
    )(eigvecs)


def scattered(values, axes):
    return lax.all_to_all(values, axes, split_axis=0, concat_axis=0, tiled=True)


def collected(parts, axes):
    groups = lax.axis_size(axes)
    total = jnp.sum(parts.reshape(groups, -1, parts.shape[1]), axis=0)
    spread = jnp.broadcast_to(total[None], (groups,) + total.shape).reshape(parts.shape)
    return lax.all_to_all(spread, axes, split_axis=0, concat_axis=0, tiled=True)


def turn(sign):
    size = lax.axis_size("x")
    pairs = []
    for x in range(size):
        for core in range(2):
            step = sign if core == 0 else -sign
            pairs.append((x * 2 + core, (x + step) % size * 2 + core))
    return pairs


def send(piece, sign):
    return lax.ppermute(piece, ("x", "core"), turn(sign))


def swap(piece, axis):
    return lax.ppermute(piece, axis, [(0, 1), (1, 0)])


def block_places():
    size = lax.axis_size("x")
    yhi, x, core = (lax.axis_index(name) for name in COL)
    places = []
    for c in (core, 1 - core):
        sign = 1 - 2 * c
        for y in (yhi, 1 - yhi):
            for step in (0, -1, 1, -2):
                places.append((y * size + lax.rem(x + sign * step + size, size)) * 2 + c)
    return jnp.stack(places).astype(jnp.int32)


def after(values, *done):
    tied = lax.optimization_barrier((*values, *done))
    return tied[: len(values)], tied[len(values) :]


def on_device(eigvecs, panels, tri_factors):
    count, block_size, depth = panels.shape
    start = (lax.axis_index(ROW) * lax.axis_size(COL) + lax.axis_index(COL)) * depth
    place = start + lax.broadcasted_iota(jnp.int32, (block_size, depth), 1)
    limit = lax.broadcasted_iota(jnp.int32, (block_size, depth), 0)
    shaped = []
    for j in range(count):
        gap = place - limit - (j + 1) * block_size
        shaped.append(jnp.where(gap < 0, 0.0, jnp.where(gap == 0, 1.0, panels[j])))
    places = block_places()

    wide = jnp.concatenate(shaped[:2], axis=0)
    slim = shaped[2]
    wide_there = swap(wide, "yhi")
    wide_near, wide_other = send(wide, 1), send(wide, -1)
    slim_near, slim_other = send(slim, 1), send(slim, -1)
    early, (wide_there, wide_other) = after((slim, slim_near, slim_other), wide_there, wide_other)
    there_near, there_other = send(wide_there, 1), send(wide_there, -1)
    slim_held = [slim, slim_near, slim_other, send(slim_near, 1)]
    slim_held += [swap(part, "yhi") for part in early]
    slim_held.append(send(slim_held[5], 1))
    wide_held = [wide, wide_near, wide_other, send(wide_near, 1), wide_there, there_near, there_other]
    wide_held.append(send(there_near, 1))
    block = columns_apart(eigvecs, lax.axis_size(COL))
    (block,), held = after((block,), *wide_held[1:], *slim_held[1:])
    wide_held[1:], slim_held[1:] = held[:7], held[7:]
    block = lax.all_to_all(block, COL, split_axis=0, concat_axis=0, tiled=True)
    pieces = list(zip(wide_held, slim_held))
    pieces += [tuple(swap(part, "core") for part in parts) for parts in pieces]

    gram = gram_of(pieces, block_size)
    size = lax.axis_size("z")
    for step in (1, 2):
        gram = gram + lax.ppermute(gram, "z", [(i, i ^ step) for i in range(size)])
    other = swap(gram, "ylo")
    parts = scattered(project(places, block, pieces), ROW)
    (other,), (parts,) = after((other,), parts)
    mixer = mix(tri_factors, gram + other)
    return apply(places, block, mixer, collected(parts, ROW), pieces)


def solution(mesh):
    fine = Mesh(mesh.devices.reshape(2, 4, 2, 4, 2), AXES)
    in_specs = (P(AXES, None), P(None, None, AXES), P())
    out_specs = P(ROW, COL)
    return jax.shard_map(on_device, mesh=fine, in_specs=in_specs, out_specs=out_specs, check_vma=False)
```

```python
import functools

import jax
import jax.numpy as jnp
from jax import lax
from jax.experimental import pallas as pl
from jax.experimental.pallas import tpu as pltpu
from jax.sharding import Mesh
from jax.sharding import PartitionSpec as P

AXES = ("ylo", "z", "yhi", "x", "core")
ROW = ("ylo", "z")
COL = ("yhi", "x", "core")


def halves(values):
    high = values.astype(jnp.bfloat16)
    low = (values - high.astype(jnp.float32)).astype(jnp.bfloat16)
    return high, low


def triple(left, right, dims):
    left_high, left_low = halves(left)
    right_high, right_low = halves(right)

    def dot(a, b):
        return lax.dot_general(a, b, (dims, ((), ())), preferred_element_type=jnp.float32)

    return dot(left_high, right_high) + (dot(left_high, right_low) + dot(left_low, right_high))


SLOTS = 4
LIMIT = pltpu.CompilerParams(vmem_limit_bytes=60 * 2**20)


def fetch_pieces(pieces, k, v_buf, v_sems):
    for i, parts in enumerate(pieces):

        @pl.when(k == i)
        def _(parts=parts, i=i):
            start = 0
            for part in parts:
                rows = part.shape[0]
                target = v_buf.at[i % SLOTS, pl.ds(start, rows)]
                pltpu.make_async_copy(part, target, v_sems.at[i % SLOTS]).start()
                start += rows


def arrive(buffer, sem):
    pltpu.make_async_copy(buffer, buffer, sem).wait()


def block_rows(ref, places, k, depth):
    return ref.at[pl.ds(pl.multiple_of(places[k] * depth, depth), depth)]


def fetch_block(places, k, e_ref, e_buf, e_sems, v_ref, v_buf, v_sems):
    slot = lax.rem(k, SLOTS)
    pltpu.make_async_copy(v_ref.at[k], v_buf.at[slot], v_sems.at[slot]).start()
    pltpu.make_async_copy(block_rows(e_ref, places, k, e_buf.shape[1]), e_buf.at[slot], e_sems.at[slot]).start()


def grouped(flat, blocks):
    size = len(flat) // blocks
    return [flat[k * size : (k + 1) * size] for k in range(blocks)]


def dot(left, right, dims):
    return lax.dot_general(left, right, (dims, ((), ())), preferred_element_type=jnp.float32)


def split_triple(left, right, dims):
    return dot(left[0], right[0], dims) + (dot(left[0], right[1], dims) + dot(left[1], right[0], dims))


def gram_kernel(blocks, size, *refs):
    flat, (g_ref, halves_ref, v_buf, h_buf, v_sems, h_sems) = refs[:-6], refs[-6:]
    pieces = grouped(flat, blocks)

    def leave(k):
        slot = lax.rem(k, SLOTS)
        return pltpu.make_async_copy(h_buf.at[slot], halves_ref.at[k], h_sems.at[slot])

    for k in range(SLOTS - 1):
        fetch_pieces(pieces, k, v_buf, v_sems)
    g_ref[...] = jnp.zeros_like(g_ref)

    @pl.loop(0, blocks)
    def _(k):
        @pl.when(k + SLOTS - 1 < blocks)
        def _():
            fetch_pieces(pieces, k + SLOTS - 1, v_buf, v_sems)

        slot = lax.rem(k, SLOTS)
        arrive(v_buf.at[slot], v_sems.at[slot])

        @pl.when(k >= SLOTS)
        def _():
            leave(k - SLOTS).wait()

        h_buf[slot, 0], h_buf[slot, 1] = halves(v_buf[slot])
        leave(k).start()
        first, second, third = (
            (h_buf[slot, 0, pl.ds(j * size, size)], h_buf[slot, 1, pl.ds(j * size, size)]) for j in range(3)
        )
        across = ((1,), (1,))
        g_ref[0] += split_triple(first, second, across)
        g_ref[1] += split_triple(first, third, across)
        g_ref[2] += split_triple(second, third, across)

    @pl.loop(blocks - SLOTS, blocks)
    def _(k):
        leave(k).wait()


def project_kernel(places, e_ref, v_ref, w_ref, e_buf, v_buf, e_sems, v_sems):
    blocks = v_ref.shape[0]
    for k in range(SLOTS - 1):
        fetch_block(places, k, e_ref, e_buf, e_sems, v_ref, v_buf, v_sems)
    w_ref[...] = jnp.zeros_like(w_ref)

    @pl.loop(0, blocks)
    def _(k):
        @pl.when(k + SLOTS - 1 < blocks)
        def _():
            fetch_block(places, k + SLOTS - 1, e_ref, e_buf, e_sems, v_ref, v_buf, v_sems)

        slot = lax.rem(k, SLOTS)
        arrive(e_buf.at[slot], e_sems.at[slot])
        arrive(v_buf.at[slot], v_sems.at[slot])
        w_ref[...] += split_triple((v_buf[slot, 0], v_buf[slot, 1]), halves(e_buf[slot]), ((1,), (0,)))


def apply_kernel(places, e_ref, m_ref, w_ref, v_ref, o_ref, e_buf, v_buf, o_buf, y_ref, e_sems, v_sems, o_sems):
    blocks = v_ref.shape[0]
    depth = e_buf.shape[1]
    for k in range(SLOTS - 1):
        fetch_block(places, k, e_ref, e_buf, e_sems, v_ref, v_buf, v_sems)
    y_ref[0], y_ref[1] = halves(triple(m_ref[...], w_ref[...], ((1,), (0,))))

    def leave(k):
        slot = lax.rem(k, SLOTS)
        return pltpu.make_async_copy(o_buf.at[slot], block_rows(o_ref, places, k, depth), o_sems.at[slot])

    @pl.loop(0, blocks)
    def _(k):
        @pl.when(k + SLOTS - 1 < blocks)
        def _():
            fetch_block(places, k + SLOTS - 1, e_ref, e_buf, e_sems, v_ref, v_buf, v_sems)

        slot = lax.rem(k, SLOTS)
        arrive(e_buf.at[slot], e_sems.at[slot])
        arrive(v_buf.at[slot], v_sems.at[slot])

        @pl.when(k >= SLOTS)
        def _():
            leave(k - SLOTS).wait()

        o_buf[slot] = e_buf[slot] - split_triple((v_buf[slot, 0], v_buf[slot, 1]), (y_ref[0], y_ref[1]), ((0,), (0,)))
        leave(k).start()

    @pl.loop(blocks - SLOTS, blocks)
    def _(k):
        leave(k).wait()


FAR = pl.BlockSpec(memory_space=pltpu.HBM)
NEAR = pl.BlockSpec(memory_space=pltpu.VMEM)
SCALARS = pl.BlockSpec(memory_space=pltpu.SMEM)


def cost(blocks, count, depth, width, passes):
    return pl.CostEstimate(
        flops=6 * blocks * count * depth * width,
        bytes_accessed=4 * blocks * depth * passes * width,
        transcendentals=0,
    )


def gram_of(pieces, size):
    blocks, count, depth = len(pieces), sum(part.shape[0] for part in pieces[0]), pieces[0][0].shape[1]
    flat = [part for parts in pieces for part in parts]
    return pl.pallas_call(
        functools.partial(gram_kernel, blocks, size),
        in_specs=[FAR] * len(flat),
        out_specs=[NEAR, FAR],
        out_shape=[
            jax.ShapeDtypeStruct((3, size, size), jnp.float32),
            jax.ShapeDtypeStruct((blocks, 2, count, depth), jnp.bfloat16),
        ],
        scratch_shapes=[
            pltpu.VMEM((SLOTS, count, depth), jnp.float32),
            pltpu.VMEM((SLOTS, 2, count, depth), jnp.bfloat16),
            pltpu.SemaphoreType.DMA((SLOTS,)),
            pltpu.SemaphoreType.DMA((SLOTS,)),
        ],
        compiler_params=LIMIT,
        cost_estimate=cost(blocks, count, depth, size, 3),
    )(*flat)


def project(places, block, vectors):
    blocks, _, count, depth = vectors.shape
    width = block.shape[1]
    return pl.pallas_call(
        project_kernel,
        in_specs=[SCALARS, FAR, FAR],
        out_specs=NEAR,
        out_shape=jax.ShapeDtypeStruct((count, width), jnp.float32),
        scratch_shapes=[
            pltpu.VMEM((SLOTS, depth, width), jnp.float32),
            pltpu.VMEM((SLOTS, 2, count, depth), jnp.bfloat16),
            pltpu.SemaphoreType.DMA((SLOTS,)),
            pltpu.SemaphoreType.DMA((SLOTS,)),
        ],
        compiler_params=LIMIT,
        cost_estimate=cost(blocks, count, depth, width, 1),
    )(places, block, vectors)


def apply(places, block, mixer, w, vectors):
    blocks, _, count, depth = vectors.shape
    width = block.shape[1]
    return pl.pallas_call(
        apply_kernel,
        in_specs=[SCALARS, FAR, NEAR, NEAR, FAR],
        out_specs=FAR,
        out_shape=jax.ShapeDtypeStruct(block.shape, jnp.float32),
        scratch_shapes=[
            pltpu.VMEM((SLOTS, depth, width), jnp.float32),
            pltpu.VMEM((SLOTS, 2, count, depth), jnp.bfloat16),
            pltpu.VMEM((SLOTS, depth, width), jnp.float32),
            pltpu.VMEM((2, count, width), jnp.bfloat16),
            pltpu.SemaphoreType.DMA((SLOTS,)),
            pltpu.SemaphoreType.DMA((SLOTS,)),
            pltpu.SemaphoreType.DMA((SLOTS,)),
        ],
        compiler_params=LIMIT,
        cost_estimate=cost(blocks, count, depth, width, 2),
    )(places, block, mixer, w, vectors)


def mix_kernel(t_ref, g_ref, m_ref):
    size = t_ref.shape[1]

    def times(left, right):
        return triple(left, right, ((1,), (0,)))

    m_ref[...] = jnp.zeros_like(m_ref)
    for j in range(3):
        m_ref[pl.ds(j * size, size), pl.ds(j * size, size)] = t_ref[j]
    middle = -times(t_ref[1], times(g_ref[2], t_ref[2]))
    m_ref[pl.ds(size, size), pl.ds(2 * size, size)] = middle
    m_ref[pl.ds(0, size), pl.ds(size, size)] = -times(t_ref[0], times(g_ref[0], t_ref[1]))
    far = times(g_ref[1], t_ref[2]) + times(g_ref[0], middle)
    m_ref[pl.ds(0, size), pl.ds(2 * size, size)] = -times(t_ref[0], far)


def mix(tri_factors, gram):
    size = 3 * tri_factors.shape[1]
    return pl.pallas_call(
        mix_kernel,
        in_specs=[NEAR, NEAR],
        out_specs=NEAR,
        out_shape=jax.ShapeDtypeStruct((size, size), jnp.float32),
        compiler_params=LIMIT,
    )(tri_factors, gram)


def columns_kernel(e_ref, o_ref, buf, in_sems, out_sems):
    blocks, depth, width = buf.shape
    arrivals = [
        pltpu.make_async_copy(e_ref.at[:, pl.ds(k * width, width)], buf.at[k], in_sems.at[k]) for k in range(blocks)
    ]
    leaves = [
        pltpu.make_async_copy(buf.at[k], o_ref.at[pl.ds(k * depth, depth)], out_sems.at[k]) for k in range(blocks)
    ]
    for copy in arrivals:
        copy.start()
    for arrival, leave in zip(arrivals, leaves):
        arrival.wait()
        leave.start()
    for leave in leaves:
        leave.wait()


def columns_apart(eigvecs, blocks):
    depth, width = eigvecs.shape[0], eigvecs.shape[1] // blocks
    return pl.pallas_call(
        columns_kernel,
        in_specs=[pl.BlockSpec(memory_space=pltpu.HBM)],
        out_specs=pl.BlockSpec(memory_space=pltpu.HBM),
        out_shape=jax.ShapeDtypeStruct((blocks * depth, width), jnp.float32),
        scratch_shapes=[
            pltpu.VMEM((blocks, depth, width), jnp.float32),
            pltpu.SemaphoreType.DMA((blocks,)),
            pltpu.SemaphoreType.DMA((blocks,)),
        ],
        compiler_params=LIMIT,
        cost_estimate=pl.CostEstimate(flops=0, bytes_accessed=8 * blocks * depth * width, transcendentals=0),
    )(eigvecs)


def scattered(values, axes):
    return lax.all_to_all(values, axes, split_axis=0, concat_axis=0, tiled=True)


def collected(parts, axes):
    groups = lax.axis_size(axes)
    total = jnp.sum(parts.reshape(groups, -1, parts.shape[1]), axis=0)
    spread = jnp.broadcast_to(total[None], (groups,) + total.shape).reshape(parts.shape)
    return lax.all_to_all(spread, axes, split_axis=0, concat_axis=0, tiled=True)


def turn(sign):
    size = lax.axis_size("x")
    pairs = []
    for x in range(size):
        for core in range(2):
            step = sign if core == 0 else -sign
            pairs.append((x * 2 + core, (x + step) % size * 2 + core))
    return pairs


def send(piece, sign):
    return lax.ppermute(piece, ("x", "core"), turn(sign))


def swap(piece, axis):
    return lax.ppermute(piece, axis, [(0, 1), (1, 0)])


def block_places():
    size = lax.axis_size("x")
    yhi, x, core = (lax.axis_index(name) for name in COL)
    places = []
    for c in (core, 1 - core):
        sign = 1 - 2 * c
        for y in (yhi, 1 - yhi):
            for step in (0, -1, 1, -2):
                places.append((y * size + lax.rem(x + sign * step + size, size)) * 2 + c)
    return jnp.stack(places).astype(jnp.int32)


def after(values, *done):
    tied = lax.optimization_barrier((*values, *done))
    return tied[: len(values)], tied[len(values) :]


def on_device(eigvecs, panels, tri_factors):
    count, block_size, depth = panels.shape
    start = (lax.axis_index(ROW) * lax.axis_size(COL) + lax.axis_index(COL)) * depth
    place = start + lax.broadcasted_iota(jnp.int32, (block_size, depth), 1)
    limit = lax.broadcasted_iota(jnp.int32, (block_size, depth), 0)
    shaped = []
    for j in range(count):
        gap = place - limit - (j + 1) * block_size
        shaped.append(jnp.where(gap < 0, 0.0, jnp.where(gap == 0, 1.0, panels[j])))
    places = block_places()

    wide = jnp.concatenate(shaped[:2], axis=0)
    slim = shaped[2]
    wide_there = swap(wide, "yhi")
    slim_near, slim_other = send(slim, 1), send(slim, -1)
    wide_near, wide_other = send(wide, 1), send(wide, -1)
    slim_far = send(slim_near, 1)
    early, (wide_there, wide_other) = after((slim, slim_near, slim_other), wide_there, wide_other)
    (wide_there,), (slim_far,) = after((wide_there,), slim_far)
    there_near, there_other = send(wide_there, 1), send(wide_there, -1)
    slim_held = [slim, slim_near, slim_other, slim_far]
    slim_held += [swap(part, "yhi") for part in (*early, slim_far)]
    wide_held = [wide, wide_near, wide_other, send(wide_near, 1), wide_there, there_near, there_other]
    wide_held.append(send(there_near, 1))
    block = columns_apart(eigvecs, lax.axis_size(COL))
    (block,), held = after((block,), *wide_held[1:], *slim_held[1:])
    wide_held[1:], slim_held[1:] = held[:7], held[7:]
    block = lax.all_to_all(block, COL, split_axis=0, concat_axis=0, tiled=True)
    pieces = list(zip(wide_held, slim_held))
    pieces += [tuple(swap(part, "core") for part in parts) for parts in pieces]

    gram, vectors = gram_of(pieces, block_size)
    size = lax.axis_size("z")
    for step in (1, 2):
        gram = gram + lax.ppermute(gram, "z", [(i, i ^ step) for i in range(size)])
    other = swap(gram, "ylo")
    parts = scattered(project(places, block, vectors), ROW)
    (other,), (parts,) = after((other,), parts)
    mixer = mix(tri_factors, gram + other)
    return apply(places, block, mixer, collected(parts, ROW), vectors)


def solution(mesh):
    fine = Mesh(mesh.devices.reshape(2, 4, 2, 4, 2), AXES)
    in_specs = (P(AXES, None), P(None, None, AXES), P())
    out_specs = P(ROW, COL)
    return jax.shard_map(on_device, mesh=fine, in_specs=in_specs, out_specs=out_specs, check_vma=False)
```

```python
import functools

import jax
import jax.numpy as jnp
from jax import lax
from jax.experimental import pallas as pl
from jax.experimental.pallas import tpu as pltpu
from jax.sharding import Mesh
from jax.sharding import PartitionSpec as P

AXES = ("ylo", "z", "yhi", "x", "core")
ROW = ("ylo", "z")
COL = ("yhi", "x", "core")


def halves(values):
    high = values.astype(jnp.bfloat16)
    low = (values - high.astype(jnp.float32)).astype(jnp.bfloat16)
    return high, low


def triple(left, right, dims):
    left_high, left_low = halves(left)
    right_high, right_low = halves(right)

    def dot(a, b):
        return lax.dot_general(a, b, (dims, ((), ())), preferred_element_type=jnp.float32)

    return dot(left_high, right_high) + (dot(left_high, right_low) + dot(left_low, right_high))


SLOTS = 4
LIMIT = pltpu.CompilerParams(vmem_limit_bytes=60 * 2**20)


def fetch_pieces(pieces, k, v_buf, v_sems):
    for i, parts in enumerate(pieces):

        @pl.when(k == i)
        def _(parts=parts, i=i):
            start = 0
            for part in parts:
                rows = part.shape[0]
                target = v_buf.at[i % SLOTS, pl.ds(start, rows)]
                pltpu.make_async_copy(part, target, v_sems.at[i % SLOTS]).start()
                start += rows


def arrive(buffer, sem):
    pltpu.make_async_copy(buffer, buffer, sem).wait()


def block_rows(ref, places, k, depth):
    return ref.at[pl.ds(pl.multiple_of(places[k] * depth, depth), depth)]


def fetch_block(places, k, e_ref, e_buf, e_sems, v_ref, v_buf, v_sems):
    slot = lax.rem(k, SLOTS)
    pltpu.make_async_copy(v_ref.at[k], v_buf.at[slot], v_sems.at[slot]).start()
    pltpu.make_async_copy(block_rows(e_ref, places, k, e_buf.shape[1]), e_buf.at[slot], e_sems.at[slot]).start()


def grouped(flat, blocks):
    size = len(flat) // blocks
    return [flat[k * size : (k + 1) * size] for k in range(blocks)]


def dot(left, right, dims):
    return lax.dot_general(left, right, (dims, ((), ())), preferred_element_type=jnp.float32)


def split_triple(left, right, dims):
    return dot(left[0], right[0], dims) + (dot(left[0], right[1], dims) + dot(left[1], right[0], dims))


def gram_kernel(blocks, size, *refs):
    flat, (g_ref, halves_ref, v_buf, h_buf, v_sems, h_sems) = refs[:-6], refs[-6:]
    pieces = grouped(flat, blocks)

    def leave(k):
        slot = lax.rem(k, SLOTS)
        return pltpu.make_async_copy(h_buf.at[slot], halves_ref.at[k], h_sems.at[slot])

    for k in range(SLOTS - 1):
        fetch_pieces(pieces, k, v_buf, v_sems)
    g_ref[...] = jnp.zeros_like(g_ref)

    @pl.loop(0, blocks)
    def _(k):
        @pl.when(k + SLOTS - 1 < blocks)
        def _():
            fetch_pieces(pieces, k + SLOTS - 1, v_buf, v_sems)

        slot = lax.rem(k, SLOTS)
        arrive(v_buf.at[slot], v_sems.at[slot])

        @pl.when(k >= SLOTS)
        def _():
            leave(k - SLOTS).wait()

        h_buf[slot, 0], h_buf[slot, 1] = halves(v_buf[slot])
        leave(k).start()
        first, second, third = (
            (h_buf[slot, 0, pl.ds(j * size, size)], h_buf[slot, 1, pl.ds(j * size, size)]) for j in range(3)
        )
        across = ((1,), (1,))
        g_ref[0] += split_triple(first, second, across)
        g_ref[1] += split_triple(first, third, across)
        g_ref[2] += split_triple(second, third, across)

    @pl.loop(blocks - SLOTS, blocks)
    def _(k):
        leave(k).wait()


def project_kernel(places, e_ref, v_ref, w_ref, e_buf, v_buf, e_sems, v_sems):
    blocks = v_ref.shape[0]
    for k in range(SLOTS - 1):
        fetch_block(places, k, e_ref, e_buf, e_sems, v_ref, v_buf, v_sems)
    w_ref[...] = jnp.zeros_like(w_ref)

    @pl.loop(0, blocks)
    def _(k):
        @pl.when(k + SLOTS - 1 < blocks)
        def _():
            fetch_block(places, k + SLOTS - 1, e_ref, e_buf, e_sems, v_ref, v_buf, v_sems)

        slot = lax.rem(k, SLOTS)
        arrive(e_buf.at[slot], e_sems.at[slot])
        arrive(v_buf.at[slot], v_sems.at[slot])
        w_ref[...] += split_triple((v_buf[slot, 0], v_buf[slot, 1]), halves(e_buf[slot]), ((1,), (0,)))


def apply_kernel(places, e_ref, m_ref, w_ref, v_ref, o_ref, e_buf, v_buf, o_buf, y_ref, e_sems, v_sems, o_sems):
    blocks = v_ref.shape[0]
    depth = e_buf.shape[1]
    for k in range(SLOTS - 1):
        fetch_block(places, k, e_ref, e_buf, e_sems, v_ref, v_buf, v_sems)
    y_ref[0], y_ref[1] = halves(triple(m_ref[...], w_ref[...], ((1,), (0,))))

    def leave(k):
        slot = lax.rem(k, SLOTS)
        return pltpu.make_async_copy(o_buf.at[slot], block_rows(o_ref, places, k, depth), o_sems.at[slot])

    @pl.loop(0, blocks)
    def _(k):
        @pl.when(k + SLOTS - 1 < blocks)
        def _():
            fetch_block(places, k + SLOTS - 1, e_ref, e_buf, e_sems, v_ref, v_buf, v_sems)

        slot = lax.rem(k, SLOTS)
        arrive(e_buf.at[slot], e_sems.at[slot])
        arrive(v_buf.at[slot], v_sems.at[slot])

        @pl.when(k >= SLOTS)
        def _():
            leave(k - SLOTS).wait()

        o_buf[slot] = e_buf[slot] - split_triple((v_buf[slot, 0], v_buf[slot, 1]), (y_ref[0], y_ref[1]), ((0,), (0,)))
        leave(k).start()

    @pl.loop(blocks - SLOTS, blocks)
    def _(k):
        leave(k).wait()


FAR = pl.BlockSpec(memory_space=pltpu.HBM)
NEAR = pl.BlockSpec(memory_space=pltpu.VMEM)
SCALARS = pl.BlockSpec(memory_space=pltpu.SMEM)


def cost(blocks, count, depth, width, passes):
    return pl.CostEstimate(
        flops=6 * blocks * count * depth * width,
        bytes_accessed=4 * blocks * depth * passes * width,
        transcendentals=0,
    )


def gram_of(pieces, size):
    blocks, count, depth = len(pieces), sum(part.shape[0] for part in pieces[0]), pieces[0][0].shape[1]
    flat = [part for parts in pieces for part in parts]
    return pl.pallas_call(
        functools.partial(gram_kernel, blocks, size),
        in_specs=[FAR] * len(flat),
        out_specs=[NEAR, FAR],
        out_shape=[
            jax.ShapeDtypeStruct((3, size, size), jnp.float32),
            jax.ShapeDtypeStruct((blocks, 2, count, depth), jnp.bfloat16),
        ],
        scratch_shapes=[
            pltpu.VMEM((SLOTS, count, depth), jnp.float32),
            pltpu.VMEM((SLOTS, 2, count, depth), jnp.bfloat16),
            pltpu.SemaphoreType.DMA((SLOTS,)),
            pltpu.SemaphoreType.DMA((SLOTS,)),
        ],
        compiler_params=LIMIT,
        cost_estimate=cost(blocks, count, depth, size, 3),
    )(*flat)


def project(places, block, vectors):
    blocks, _, count, depth = vectors.shape
    width = block.shape[1]
    return pl.pallas_call(
        project_kernel,
        in_specs=[SCALARS, FAR, FAR],
        out_specs=NEAR,
        out_shape=jax.ShapeDtypeStruct((count, width), jnp.float32),
        scratch_shapes=[
            pltpu.VMEM((SLOTS, depth, width), jnp.float32),
            pltpu.VMEM((SLOTS, 2, count, depth), jnp.bfloat16),
            pltpu.SemaphoreType.DMA((SLOTS,)),
            pltpu.SemaphoreType.DMA((SLOTS,)),
        ],
        compiler_params=LIMIT,
        cost_estimate=cost(blocks, count, depth, width, 1),
    )(places, block, vectors)


def apply(places, block, mixer, w, vectors):
    blocks, _, count, depth = vectors.shape
    width = block.shape[1]
    return pl.pallas_call(
        apply_kernel,
        in_specs=[SCALARS, FAR, NEAR, NEAR, FAR],
        out_specs=FAR,
        out_shape=jax.ShapeDtypeStruct(block.shape, jnp.float32),
        scratch_shapes=[
            pltpu.VMEM((SLOTS, depth, width), jnp.float32),
            pltpu.VMEM((SLOTS, 2, count, depth), jnp.bfloat16),
            pltpu.VMEM((SLOTS, depth, width), jnp.float32),
            pltpu.VMEM((2, count, width), jnp.bfloat16),
            pltpu.SemaphoreType.DMA((SLOTS,)),
            pltpu.SemaphoreType.DMA((SLOTS,)),
            pltpu.SemaphoreType.DMA((SLOTS,)),
        ],
        compiler_params=LIMIT,
        cost_estimate=cost(blocks, count, depth, width, 2),
    )(places, block, mixer, w, vectors)


def mix_kernel(t_ref, g_ref, m_ref):
    size = t_ref.shape[1]

    def times(left, right):
        return triple(left, right, ((1,), (0,)))

    m_ref[...] = jnp.zeros_like(m_ref)
    for j in range(3):
        m_ref[pl.ds(j * size, size), pl.ds(j * size, size)] = t_ref[j]
    middle = -times(t_ref[1], times(g_ref[2], t_ref[2]))
    m_ref[pl.ds(size, size), pl.ds(2 * size, size)] = middle
    m_ref[pl.ds(0, size), pl.ds(size, size)] = -times(t_ref[0], times(g_ref[0], t_ref[1]))
    far = times(g_ref[1], t_ref[2]) + times(g_ref[0], middle)
    m_ref[pl.ds(0, size), pl.ds(2 * size, size)] = -times(t_ref[0], far)


def mix(tri_factors, gram):
    size = 3 * tri_factors.shape[1]
    return pl.pallas_call(
        mix_kernel,
        in_specs=[NEAR, NEAR],
        out_specs=NEAR,
        out_shape=jax.ShapeDtypeStruct((size, size), jnp.float32),
        compiler_params=LIMIT,
    )(tri_factors, gram)


def columns_kernel(e_ref, o_ref, buf, in_sems, out_sems):
    blocks, depth, width = buf.shape
    arrivals = [
        pltpu.make_async_copy(e_ref.at[:, pl.ds(k * width, width)], buf.at[k], in_sems.at[k]) for k in range(blocks)
    ]
    leaves = [
        pltpu.make_async_copy(buf.at[k], o_ref.at[pl.ds(k * depth, depth)], out_sems.at[k]) for k in range(blocks)
    ]
    for copy in arrivals:
        copy.start()
    for arrival, leave in zip(arrivals, leaves):
        arrival.wait()
        leave.start()
    for leave in leaves:
        leave.wait()


def columns_apart(eigvecs, blocks):
    depth, width = eigvecs.shape[0], eigvecs.shape[1] // blocks
    return pl.pallas_call(
        columns_kernel,
        in_specs=[pl.BlockSpec(memory_space=pltpu.HBM)],
        out_specs=pl.BlockSpec(memory_space=pltpu.HBM),
        out_shape=jax.ShapeDtypeStruct((blocks * depth, width), jnp.float32),
        scratch_shapes=[
            pltpu.VMEM((blocks, depth, width), jnp.float32),
            pltpu.SemaphoreType.DMA((blocks,)),
            pltpu.SemaphoreType.DMA((blocks,)),
        ],
        compiler_params=LIMIT,
        cost_estimate=pl.CostEstimate(flops=0, bytes_accessed=8 * blocks * depth * width, transcendentals=0),
    )(eigvecs)


def scattered(values, axes):
    return lax.all_to_all(values, axes, split_axis=0, concat_axis=0, tiled=True)


def collected(parts, axes):
    groups = lax.axis_size(axes)
    total = jnp.sum(parts.reshape(groups, -1, parts.shape[1]), axis=0)
    spread = jnp.broadcast_to(total[None], (groups,) + total.shape).reshape(parts.shape)
    return lax.all_to_all(spread, axes, split_axis=0, concat_axis=0, tiled=True)


def turn(sign):
    size = lax.axis_size("x")
    pairs = []
    for x in range(size):
        for core in range(2):
            step = sign if core == 0 else -sign
            pairs.append((x * 2 + core, (x + step) % size * 2 + core))
    return pairs


def send(piece, sign):
    return lax.ppermute(piece, ("x", "core"), turn(sign))


def swap(piece, axis):
    return lax.ppermute(piece, axis, [(0, 1), (1, 0)])


def block_places():
    size = lax.axis_size("x")
    yhi, x, core = (lax.axis_index(name) for name in COL)
    places = []
    for c in (core, 1 - core):
        sign = 1 - 2 * c
        for y in (yhi, 1 - yhi):
            for step in (0, -1, 1, -2):
                places.append((y * size + lax.rem(x + sign * step + size, size)) * 2 + c)
    return jnp.stack(places).astype(jnp.int32)


def after(values, *done):
    tied = lax.optimization_barrier((*values, *done))
    return tied[: len(values)], tied[len(values) :]


def on_device(eigvecs, panels, tri_factors):
    count, block_size, depth = panels.shape
    start = (lax.axis_index(ROW) * lax.axis_size(COL) + lax.axis_index(COL)) * depth
    place = start + lax.broadcasted_iota(jnp.int32, (block_size, depth), 1)
    limit = lax.broadcasted_iota(jnp.int32, (block_size, depth), 0)
    shaped = []
    for j in range(count):
        gap = place - limit - (j + 1) * block_size
        shaped.append(jnp.where(gap < 0, 0.0, jnp.where(gap == 0, 1.0, panels[j])))
    places = block_places()

    wide = jnp.concatenate(shaped[:2], axis=0)
    slim = shaped[2]
    wide_there = swap(wide, "yhi")
    slim_near, slim_other = send(slim, 1), send(slim, -1)
    wide_near, wide_other = send(wide, 1), send(wide, -1)
    slim_far = send(slim_near, 1)
    early, (wide_there, wide_other) = after((slim, slim_near, slim_other), wide_there, wide_other)
    (wide_there,), (slim_far,) = after((wide_there,), slim_far)
    there_near, there_other = send(wide_there, 1), send(wide_there, -1)
    both = swap(jnp.concatenate(early[1:], axis=0), "yhi")
    slim_there, far_there = swap(early[0], "yhi"), swap(slim_far, "yhi")
    slim_held = [slim, slim_near, slim_other, slim_far]
    wide_held = [wide, wide_near, wide_other, send(wide_near, 1), wide_there, there_near, there_other]
    wide_held.append(send(there_near, 1))
    block = columns_apart(eigvecs, lax.axis_size(COL))
    (block,), held = after((block,), *wide_held[1:], *slim_held[1:], slim_there, both, far_there)
    wide_held[1:], slim_held[1:] = held[:7], held[7:10]
    slim_there, both, far_there = held[10:]
    slim_held += [slim_there, both[:block_size], both[block_size:], far_there]
    block = lax.all_to_all(block, COL, split_axis=0, concat_axis=0, tiled=True)
    pieces = list(zip(wide_held, slim_held))
    pieces += [tuple(swap(part, "core") for part in parts) for parts in pieces]

    gram, vectors = gram_of(pieces, block_size)
    size = lax.axis_size("z")
    for step in (1, 2):
        gram = gram + lax.ppermute(gram, "z", [(i, i ^ step) for i in range(size)])
    other = swap(gram, "ylo")
    parts = scattered(project(places, block, vectors), ROW)
    (other,), (parts,) = after((other,), parts)
    mixer = mix(tri_factors, gram + other)
    return apply(places, block, mixer, collected(parts, ROW), vectors)


def solution(mesh):
    fine = Mesh(mesh.devices.reshape(2, 4, 2, 4, 2), AXES)
    in_specs = (P(AXES, None), P(None, None, AXES), P())
    out_specs = P(ROW, COL)
    return jax.shard_map(on_device, mesh=fine, in_specs=in_specs, out_specs=out_specs, check_vma=False)
```

```python
import functools

import jax
import jax.numpy as jnp
from jax import lax
from jax.experimental import pallas as pl
from jax.experimental.pallas import tpu as pltpu
from jax.sharding import Mesh
from jax.sharding import PartitionSpec as P

AXES = ("ylo", "z", "yhi", "x", "core")
ROW = ("ylo", "z")
COL = ("yhi", "x", "core")


def halves(values):
    high = values.astype(jnp.bfloat16)
    low = (values - high.astype(jnp.float32)).astype(jnp.bfloat16)
    return high, low


def triple(left, right, dims):
    left_high, left_low = halves(left)
    right_high, right_low = halves(right)

    def dot(a, b):
        return lax.dot_general(a, b, (dims, ((), ())), preferred_element_type=jnp.float32)

    return dot(left_high, right_high) + (dot(left_high, right_low) + dot(left_low, right_high))


SLOTS = 4
LIMIT = pltpu.CompilerParams(vmem_limit_bytes=60 * 2**20)
SMALLER = pltpu.CompilerParams(vmem_limit_bytes=48 * 2**20)


def fetch_pieces(pieces, k, v_buf, v_sems):
    for i, parts in enumerate(pieces):

        @pl.when(k == i)
        def _(parts=parts, i=i):
            start = 0
            for part in parts:
                rows = part.shape[0]
                target = v_buf.at[i % SLOTS, pl.ds(start, rows)]
                pltpu.make_async_copy(part, target, v_sems.at[i % SLOTS]).start()
                start += rows


def arrive(buffer, sem):
    pltpu.make_async_copy(buffer, buffer, sem).wait()


def block_rows(ref, places, k, depth):
    return ref.at[pl.ds(pl.multiple_of(places[k] * depth, depth), depth)]


def fetch_block(places, k, e_ref, e_buf, e_sems, v_ref, v_buf, v_sems):
    slot = lax.rem(k, SLOTS)
    pltpu.make_async_copy(v_ref.at[k], v_buf.at[slot], v_sems.at[slot]).start()
    pltpu.make_async_copy(block_rows(e_ref, places, k, e_buf.shape[1]), e_buf.at[slot], e_sems.at[slot]).start()


def grouped(flat, blocks):
    size = len(flat) // blocks
    return [flat[k * size : (k + 1) * size] for k in range(blocks)]


def dot(left, right, dims):
    return lax.dot_general(left, right, (dims, ((), ())), preferred_element_type=jnp.float32)


def split_triple(left, right, dims):
    return dot(left[0], right[0], dims) + (dot(left[0], right[1], dims) + dot(left[1], right[0], dims))


def gram_kernel(blocks, size, *refs):
    flat, (g_ref, halves_ref, v_buf, h_buf, v_sems, h_sems) = refs[:-6], refs[-6:]
    pieces = grouped(flat, blocks)

    def leave(k):
        slot = lax.rem(k, SLOTS)
        return pltpu.make_async_copy(h_buf.at[slot], halves_ref.at[k], h_sems.at[slot])

    for k in range(SLOTS - 1):
        fetch_pieces(pieces, k, v_buf, v_sems)
    g_ref[...] = jnp.zeros_like(g_ref)

    @pl.loop(0, blocks)
    def _(k):
        @pl.when(k + SLOTS - 1 < blocks)
        def _():
            fetch_pieces(pieces, k + SLOTS - 1, v_buf, v_sems)

        slot = lax.rem(k, SLOTS)
        arrive(v_buf.at[slot], v_sems.at[slot])

        @pl.when(k >= SLOTS)
        def _():
            leave(k - SLOTS).wait()

        h_buf[slot, 0], h_buf[slot, 1] = halves(v_buf[slot])
        leave(k).start()
        first, second, third = (
            (h_buf[slot, 0, pl.ds(j * size, size)], h_buf[slot, 1, pl.ds(j * size, size)]) for j in range(3)
        )
        across = ((1,), (1,))
        g_ref[0] += split_triple(first, second, across)
        g_ref[1] += split_triple(first, third, across)
        g_ref[2] += split_triple(second, third, across)

    @pl.loop(blocks - SLOTS, blocks)
    def _(k):
        leave(k).wait()


def project_kernel(places, e_ref, v_ref, w_ref, e_buf, v_buf, e_sems, v_sems):
    blocks = v_ref.shape[0]
    for k in range(SLOTS - 1):
        fetch_block(places, k, e_ref, e_buf, e_sems, v_ref, v_buf, v_sems)
    w_ref[...] = jnp.zeros_like(w_ref)

    @pl.loop(0, blocks)
    def _(k):
        @pl.when(k + SLOTS - 1 < blocks)
        def _():
            fetch_block(places, k + SLOTS - 1, e_ref, e_buf, e_sems, v_ref, v_buf, v_sems)

        slot = lax.rem(k, SLOTS)
        arrive(e_buf.at[slot], e_sems.at[slot])
        arrive(v_buf.at[slot], v_sems.at[slot])
        w_ref[...] += split_triple((v_buf[slot, 0], v_buf[slot, 1]), halves(e_buf[slot]), ((1,), (0,)))


def apply_kernel(
    places, e_ref, m_ref, w_ref, v_ref, o_ref, w_buf, e_buf, v_buf, o_buf, y_ref, w_sem, e_sems, v_sems, o_sems
):
    blocks = v_ref.shape[0]
    depth = e_buf.shape[1]
    sums = pltpu.make_async_copy(w_ref, w_buf, w_sem)
    sums.start()
    for k in range(SLOTS - 1):
        fetch_block(places, k, e_ref, e_buf, e_sems, v_ref, v_buf, v_sems)
    sums.wait()
    y_ref[0], y_ref[1] = halves(triple(m_ref[...], w_buf[...], ((1,), (0,))))

    def leave(k):
        slot = lax.rem(k, SLOTS)
        return pltpu.make_async_copy(o_buf.at[slot], block_rows(o_ref, places, k, depth), o_sems.at[slot])

    @pl.loop(0, blocks)
    def _(k):
        @pl.when(k + SLOTS - 1 < blocks)
        def _():
            fetch_block(places, k + SLOTS - 1, e_ref, e_buf, e_sems, v_ref, v_buf, v_sems)

        slot = lax.rem(k, SLOTS)
        arrive(e_buf.at[slot], e_sems.at[slot])
        arrive(v_buf.at[slot], v_sems.at[slot])

        @pl.when(k >= SLOTS)
        def _():
            leave(k - SLOTS).wait()

        o_buf[slot] = e_buf[slot] - split_triple((v_buf[slot, 0], v_buf[slot, 1]), (y_ref[0], y_ref[1]), ((0,), (0,)))
        leave(k).start()

    @pl.loop(blocks - SLOTS, blocks)
    def _(k):
        leave(k).wait()


FAR = pl.BlockSpec(memory_space=pltpu.HBM)
NEAR = pl.BlockSpec(memory_space=pltpu.VMEM)
SCALARS = pl.BlockSpec(memory_space=pltpu.SMEM)


def cost(blocks, count, depth, width, passes):
    return pl.CostEstimate(
        flops=6 * blocks * count * depth * width,
        bytes_accessed=4 * blocks * depth * passes * width,
        transcendentals=0,
    )


def gram_of(pieces, size):
    blocks, count, depth = len(pieces), sum(part.shape[0] for part in pieces[0]), pieces[0][0].shape[1]
    flat = [part for parts in pieces for part in parts]
    return pl.pallas_call(
        functools.partial(gram_kernel, blocks, size),
        in_specs=[FAR] * len(flat),
        out_specs=[NEAR, FAR],
        out_shape=[
            jax.ShapeDtypeStruct((3, size, size), jnp.float32),
            jax.ShapeDtypeStruct((blocks, 2, count, depth), jnp.bfloat16),
        ],
        scratch_shapes=[
            pltpu.VMEM((SLOTS, count, depth), jnp.float32),
            pltpu.VMEM((SLOTS, 2, count, depth), jnp.bfloat16),
            pltpu.SemaphoreType.DMA((SLOTS,)),
            pltpu.SemaphoreType.DMA((SLOTS,)),
        ],
        compiler_params=LIMIT,
        cost_estimate=cost(blocks, count, depth, size, 3),
    )(*flat)


def project(places, block, vectors):
    blocks, _, count, depth = vectors.shape
    width = block.shape[1]
    return pl.pallas_call(
        project_kernel,
        in_specs=[SCALARS, FAR, FAR],
        out_specs=NEAR,
        out_shape=jax.ShapeDtypeStruct((count, width), jnp.float32),
        scratch_shapes=[
            pltpu.VMEM((SLOTS, depth, width), jnp.float32),
            pltpu.VMEM((SLOTS, 2, count, depth), jnp.bfloat16),
            pltpu.SemaphoreType.DMA((SLOTS,)),
            pltpu.SemaphoreType.DMA((SLOTS,)),
        ],
        compiler_params=LIMIT,
        cost_estimate=cost(blocks, count, depth, width, 1),
    )(places, block, vectors)


def apply(places, block, mixer, w, vectors):
    blocks, _, count, depth = vectors.shape
    width = block.shape[1]
    return pl.pallas_call(
        apply_kernel,
        in_specs=[SCALARS, FAR, NEAR, pl.BlockSpec(memory_space=pl.ANY), FAR],
        out_specs=FAR,
        out_shape=jax.ShapeDtypeStruct(block.shape, jnp.float32),
        scratch_shapes=[
            pltpu.VMEM((count, width), jnp.float32),
            pltpu.VMEM((SLOTS, depth, width), jnp.float32),
            pltpu.VMEM((SLOTS, 2, count, depth), jnp.bfloat16),
            pltpu.VMEM((SLOTS, depth, width), jnp.float32),
            pltpu.VMEM((2, count, width), jnp.bfloat16),
            pltpu.SemaphoreType.DMA,
            pltpu.SemaphoreType.DMA((SLOTS,)),
            pltpu.SemaphoreType.DMA((SLOTS,)),
            pltpu.SemaphoreType.DMA((SLOTS,)),
        ],
        compiler_params=SMALLER,
        cost_estimate=cost(blocks, count, depth, width, 2),
    )(places, block, mixer, w, vectors)


def mix_kernel(t_ref, g_ref, m_ref):
    size = t_ref.shape[1]

    def times(left, right):
        return triple(left, right, ((1,), (0,)))

    m_ref[...] = jnp.zeros_like(m_ref)
    for j in range(3):
        m_ref[pl.ds(j * size, size), pl.ds(j * size, size)] = t_ref[j]
    middle = -times(t_ref[1], times(g_ref[2], t_ref[2]))
    m_ref[pl.ds(size, size), pl.ds(2 * size, size)] = middle
    m_ref[pl.ds(0, size), pl.ds(size, size)] = -times(t_ref[0], times(g_ref[0], t_ref[1]))
    far = times(g_ref[1], t_ref[2]) + times(g_ref[0], middle)
    m_ref[pl.ds(0, size), pl.ds(2 * size, size)] = -times(t_ref[0], far)


def mix(tri_factors, gram):
    size = 3 * tri_factors.shape[1]
    return pl.pallas_call(
        mix_kernel,
        in_specs=[NEAR, NEAR],
        out_specs=NEAR,
        out_shape=jax.ShapeDtypeStruct((size, size), jnp.float32),
        compiler_params=SMALLER,
    )(tri_factors, gram)


def columns_kernel(e_ref, o_ref, buf, in_sems, out_sems):
    blocks, depth, width = buf.shape
    arrivals = [
        pltpu.make_async_copy(e_ref.at[:, pl.ds(k * width, width)], buf.at[k], in_sems.at[k]) for k in range(blocks)
    ]
    leaves = [
        pltpu.make_async_copy(buf.at[k], o_ref.at[pl.ds(k * depth, depth)], out_sems.at[k]) for k in range(blocks)
    ]
    for copy in arrivals:
        copy.start()
    for arrival, leave in zip(arrivals, leaves):
        arrival.wait()
        leave.start()
    for leave in leaves:
        leave.wait()


def columns_apart(eigvecs, blocks):
    depth, width = eigvecs.shape[0], eigvecs.shape[1] // blocks
    return pl.pallas_call(
        columns_kernel,
        in_specs=[pl.BlockSpec(memory_space=pltpu.HBM)],
        out_specs=pl.BlockSpec(memory_space=pltpu.HBM),
        out_shape=jax.ShapeDtypeStruct((blocks * depth, width), jnp.float32),
        scratch_shapes=[
            pltpu.VMEM((blocks, depth, width), jnp.float32),
            pltpu.SemaphoreType.DMA((blocks,)),
            pltpu.SemaphoreType.DMA((blocks,)),
        ],
        compiler_params=LIMIT,
        cost_estimate=pl.CostEstimate(flops=0, bytes_accessed=8 * blocks * depth * width, transcendentals=0),
    )(eigvecs)


def scattered(values, axes):
    return lax.all_to_all(values, axes, split_axis=0, concat_axis=0, tiled=True)


def collected(parts, axes):
    groups = lax.axis_size(axes)
    total = jnp.sum(parts.reshape(groups, -1, parts.shape[1]), axis=0)
    spread = jnp.broadcast_to(total[None], (groups,) + total.shape).reshape(parts.shape)
    return lax.all_to_all(spread, axes, split_axis=0, concat_axis=0, tiled=True)


def turn(sign):
    size = lax.axis_size("x")
    pairs = []
    for x in range(size):
        for core in range(2):
            step = sign if core == 0 else -sign
            pairs.append((x * 2 + core, (x + step) % size * 2 + core))
    return pairs


def send(piece, sign):
    return lax.ppermute(piece, ("x", "core"), turn(sign))


def swap(piece, axis):
    return lax.ppermute(piece, axis, [(0, 1), (1, 0)])


def block_places():
    size = lax.axis_size("x")
    yhi, x, core = (lax.axis_index(name) for name in COL)
    places = []
    for c in (core, 1 - core):
        sign = 1 - 2 * c
        for y in (yhi, 1 - yhi):
            for step in (0, -1, 1, -2):
                places.append((y * size + lax.rem(x + sign * step + size, size)) * 2 + c)
    return jnp.stack(places).astype(jnp.int32)


def after(values, *done):
    tied = lax.optimization_barrier((*values, *done))
    return tied[: len(values)], tied[len(values) :]


def on_device(eigvecs, panels, tri_factors):
    count, block_size, depth = panels.shape
    start = (lax.axis_index(ROW) * lax.axis_size(COL) + lax.axis_index(COL)) * depth
    place = start + lax.broadcasted_iota(jnp.int32, (block_size, depth), 1)
    limit = lax.broadcasted_iota(jnp.int32, (block_size, depth), 0)
    shaped = []
    for j in range(count):
        gap = place - limit - (j + 1) * block_size
        shaped.append(jnp.where(gap < 0, 0.0, jnp.where(gap == 0, 1.0, panels[j])))
    places = block_places()

    wide = jnp.concatenate(shaped[:2], axis=0)
    slim = shaped[2]
    wide_there = swap(wide, "yhi")
    slim_near, slim_other = send(slim, 1), send(slim, -1)
    wide_near, wide_other = send(wide, 1), send(wide, -1)
    slim_far = send(slim_near, 1)
    early, (wide_there, wide_other) = after((slim, slim_near, slim_other), wide_there, wide_other)
    (wide_there,), (slim_far,) = after((wide_there,), slim_far)
    there_near, there_other = send(wide_there, 1), send(wide_there, -1)
    both = swap(jnp.concatenate(early[1:], axis=0), "yhi")
    slim_there, far_there = swap(early[0], "yhi"), swap(slim_far, "yhi")
    slim_held = [slim, slim_near, slim_other, slim_far]
    wide_held = [wide, wide_near, wide_other, send(wide_near, 1), wide_there, there_near, there_other]
    wide_held.append(send(there_near, 1))
    block = columns_apart(eigvecs, lax.axis_size(COL))
    (block,), held = after((block,), *wide_held[1:], *slim_held[1:], slim_there, both, far_there)
    wide_held[1:], slim_held[1:] = held[:7], held[7:10]
    slim_there, both, far_there = held[10:]
    slim_held += [slim_there, both[:block_size], both[block_size:], far_there]
    block = lax.all_to_all(block, COL, split_axis=0, concat_axis=0, tiled=True)
    pieces = list(zip(wide_held, slim_held))
    pieces += [tuple(swap(part, "core") for part in parts) for parts in pieces]

    gram, vectors = gram_of(pieces, block_size)
    size = lax.axis_size("z")
    for step in (1, 2):
        gram = gram + lax.ppermute(gram, "z", [(i, i ^ step) for i in range(size)])
    other = swap(gram, "ylo")
    parts = scattered(project(places, block, vectors), ROW)
    (other,), (parts,) = after((other,), parts)
    mixer = mix(tri_factors, gram + other)
    return apply(places, block, mixer, collected(parts, ROW), vectors)


def solution(mesh):
    fine = Mesh(mesh.devices.reshape(2, 4, 2, 4, 2), AXES)
    in_specs = (P(AXES, None), P(None, None, AXES), P())
    out_specs = P(ROW, COL)
    return jax.shard_map(on_device, mesh=fine, in_specs=in_specs, out_specs=out_specs, check_vma=False)
```

```python
import functools

import jax
import jax.numpy as jnp
from jax import lax
from jax.experimental import pallas as pl
from jax.experimental.pallas import tpu as pltpu
from jax.sharding import Mesh
from jax.sharding import PartitionSpec as P

AXES = ("ylo", "z", "yhi", "x", "core")
ROW = ("ylo", "z")
COL = ("yhi", "x", "core")


def halves(values):
    high = values.astype(jnp.bfloat16)
    low = (values - high.astype(jnp.float32)).astype(jnp.bfloat16)
    return high, low


def triple(left, right, dims):
    left_high, left_low = halves(left)
    right_high, right_low = halves(right)

    def dot(a, b):
        return lax.dot_general(a, b, (dims, ((), ())), preferred_element_type=jnp.float32)

    return dot(left_high, right_high) + (dot(left_high, right_low) + dot(left_low, right_high))


SLOTS = 4
LIMIT = pltpu.CompilerParams(vmem_limit_bytes=48 * 2**20)


def fetch_pieces(pieces, k, v_buf, v_sems):
    for i, parts in enumerate(pieces):

        @pl.when(k == i)
        def _(parts=parts, i=i):
            start = 0
            for part in parts:
                rows = part.shape[0]
                target = v_buf.at[i % SLOTS, pl.ds(start, rows)]
                pltpu.make_async_copy(part, target, v_sems.at[i % SLOTS]).start()
                start += rows


def arrive(buffer, sem):
    pltpu.make_async_copy(buffer, buffer, sem).wait()


def block_rows(ref, places, k, depth):
    return ref.at[pl.ds(pl.multiple_of(places[k] * depth, depth), depth)]


def fetch_block(places, k, e_ref, e_buf, e_sems, v_ref, v_buf, v_sems):
    slot = lax.rem(k, SLOTS)
    pltpu.make_async_copy(v_ref.at[k], v_buf.at[slot], v_sems.at[slot]).start()
    pltpu.make_async_copy(block_rows(e_ref, places, k, e_buf.shape[1]), e_buf.at[slot], e_sems.at[slot]).start()


def grouped(flat, blocks):
    size = len(flat) // blocks
    return [flat[k * size : (k + 1) * size] for k in range(blocks)]


def dot(left, right, dims):
    return lax.dot_general(left, right, (dims, ((), ())), preferred_element_type=jnp.float32)


def split_triple(left, right, dims):
    return dot(left[0], right[0], dims) + (dot(left[0], right[1], dims) + dot(left[1], right[0], dims))


def gram_kernel(blocks, size, *refs):
    flat, (g_ref, halves_ref, v_buf, h_buf, v_sems, h_sems) = refs[:-6], refs[-6:]
    pieces = grouped(flat, blocks)

    def leave(k):
        slot = lax.rem(k, SLOTS)
        return pltpu.make_async_copy(h_buf.at[slot], halves_ref.at[k], h_sems.at[slot])

    for k in range(SLOTS - 1):
        fetch_pieces(pieces, k, v_buf, v_sems)
    g_ref[...] = jnp.zeros_like(g_ref)

    @pl.loop(0, blocks)
    def _(k):
        @pl.when(k + SLOTS - 1 < blocks)
        def _():
            fetch_pieces(pieces, k + SLOTS - 1, v_buf, v_sems)

        slot = lax.rem(k, SLOTS)
        arrive(v_buf.at[slot], v_sems.at[slot])

        @pl.when(k >= SLOTS)
        def _():
            leave(k - SLOTS).wait()

        h_buf[slot, 0], h_buf[slot, 1] = halves(v_buf[slot])
        leave(k).start()
        first, second, third = (
            (h_buf[slot, 0, pl.ds(j * size, size)], h_buf[slot, 1, pl.ds(j * size, size)]) for j in range(3)
        )
        across = ((1,), (1,))
        g_ref[0] += split_triple(first, second, across)
        g_ref[1] += split_triple(first, third, across)
        g_ref[2] += split_triple(second, third, across)

    @pl.loop(blocks - SLOTS, blocks)
    def _(k):
        leave(k).wait()


def project_kernel(places, e_ref, v_ref, w_ref, e_buf, v_buf, e_sems, v_sems):
    blocks = v_ref.shape[0]
    for k in range(SLOTS - 1):
        fetch_block(places, k, e_ref, e_buf, e_sems, v_ref, v_buf, v_sems)
    w_ref[...] = jnp.zeros_like(w_ref)

    @pl.loop(0, blocks)
    def _(k):
        @pl.when(k + SLOTS - 1 < blocks)
        def _():
            fetch_block(places, k + SLOTS - 1, e_ref, e_buf, e_sems, v_ref, v_buf, v_sems)

        slot = lax.rem(k, SLOTS)
        arrive(e_buf.at[slot], e_sems.at[slot])
        arrive(v_buf.at[slot], v_sems.at[slot])
        w_ref[...] += split_triple((v_buf[slot, 0], v_buf[slot, 1]), halves(e_buf[slot]), ((1,), (0,)))


def apply_kernel(
    places, e_ref, m_ref, w_ref, v_ref, o_ref, w_buf, e_buf, v_buf, o_buf, y_ref, w_sem, e_sems, v_sems, o_sems
):
    blocks = v_ref.shape[0]
    depth = e_buf.shape[1]
    sums = pltpu.make_async_copy(w_ref, w_buf, w_sem)
    sums.start()
    for k in range(SLOTS - 1):
        fetch_block(places, k, e_ref, e_buf, e_sems, v_ref, v_buf, v_sems)
    sums.wait()
    y_ref[0], y_ref[1] = halves(triple(m_ref[...], w_buf[...], ((1,), (0,))))

    def leave(k):
        slot = lax.rem(k, SLOTS)
        return pltpu.make_async_copy(o_buf.at[slot], block_rows(o_ref, places, k, depth), o_sems.at[slot])

    @pl.loop(0, blocks)
    def _(k):
        @pl.when(k + SLOTS - 1 < blocks)
        def _():
            fetch_block(places, k + SLOTS - 1, e_ref, e_buf, e_sems, v_ref, v_buf, v_sems)

        slot = lax.rem(k, SLOTS)
        arrive(e_buf.at[slot], e_sems.at[slot])
        arrive(v_buf.at[slot], v_sems.at[slot])

        @pl.when(k >= SLOTS)
        def _():
            leave(k - SLOTS).wait()

        o_buf[slot] = e_buf[slot] - split_triple((v_buf[slot, 0], v_buf[slot, 1]), (y_ref[0], y_ref[1]), ((0,), (0,)))
        leave(k).start()

    @pl.loop(blocks - SLOTS, blocks)
    def _(k):
        leave(k).wait()


FAR = pl.BlockSpec(memory_space=pltpu.HBM)
NEAR = pl.BlockSpec(memory_space=pltpu.VMEM)
SCALARS = pl.BlockSpec(memory_space=pltpu.SMEM)


def cost(blocks, count, depth, width, passes):
    return pl.CostEstimate(
        flops=6 * blocks * count * depth * width,
        bytes_accessed=4 * blocks * depth * passes * width,
        transcendentals=0,
    )


def gram_of(pieces, size):
    blocks, count, depth = len(pieces), sum(part.shape[0] for part in pieces[0]), pieces[0][0].shape[1]
    flat = [part for parts in pieces for part in parts]
    return pl.pallas_call(
        functools.partial(gram_kernel, blocks, size),
        in_specs=[FAR] * len(flat),
        out_specs=[NEAR, FAR],
        out_shape=[
            jax.ShapeDtypeStruct((3, size, size), jnp.float32),
            jax.ShapeDtypeStruct((blocks, 2, count, depth), jnp.bfloat16),
        ],
        scratch_shapes=[
            pltpu.VMEM((SLOTS, count, depth), jnp.float32),
            pltpu.VMEM((SLOTS, 2, count, depth), jnp.bfloat16),
            pltpu.SemaphoreType.DMA((SLOTS,)),
            pltpu.SemaphoreType.DMA((SLOTS,)),
        ],
        compiler_params=LIMIT,
        cost_estimate=cost(blocks, count, depth, size, 3),
    )(*flat)


def project(places, block, vectors):
    blocks, _, count, depth = vectors.shape
    width = block.shape[1]
    return pl.pallas_call(
        project_kernel,
        in_specs=[SCALARS, FAR, FAR],
        out_specs=NEAR,
        out_shape=jax.ShapeDtypeStruct((count, width), jnp.float32),
        scratch_shapes=[
            pltpu.VMEM((SLOTS, depth, width), jnp.float32),
            pltpu.VMEM((SLOTS, 2, count, depth), jnp.bfloat16),
            pltpu.SemaphoreType.DMA((SLOTS,)),
            pltpu.SemaphoreType.DMA((SLOTS,)),
        ],
        compiler_params=LIMIT,
        cost_estimate=cost(blocks, count, depth, width, 1),
    )(places, block, vectors)


def apply(places, block, mixer, w, vectors):
    blocks, _, count, depth = vectors.shape
    width = block.shape[1]
    return pl.pallas_call(
        apply_kernel,
        in_specs=[SCALARS, FAR, NEAR, pl.BlockSpec(memory_space=pl.ANY), FAR],
        out_specs=FAR,
        out_shape=jax.ShapeDtypeStruct(block.shape, jnp.float32),
        scratch_shapes=[
            pltpu.VMEM((count, width), jnp.float32),
            pltpu.VMEM((SLOTS, depth, width), jnp.float32),
            pltpu.VMEM((SLOTS, 2, count, depth), jnp.bfloat16),
            pltpu.VMEM((SLOTS, depth, width), jnp.float32),
            pltpu.VMEM((2, count, width), jnp.bfloat16),
            pltpu.SemaphoreType.DMA,
            pltpu.SemaphoreType.DMA((SLOTS,)),
            pltpu.SemaphoreType.DMA((SLOTS,)),
            pltpu.SemaphoreType.DMA((SLOTS,)),
        ],
        compiler_params=LIMIT,
        cost_estimate=cost(blocks, count, depth, width, 2),
    )(places, block, mixer, w, vectors)


def mix_kernel(t_ref, g_ref, m_ref):
    size = t_ref.shape[1]

    def times(left, right):
        return triple(left, right, ((1,), (0,)))

    m_ref[...] = jnp.zeros_like(m_ref)
    for j in range(3):
        m_ref[pl.ds(j * size, size), pl.ds(j * size, size)] = t_ref[j]
    middle = -times(t_ref[1], times(g_ref[2], t_ref[2]))
    m_ref[pl.ds(size, size), pl.ds(2 * size, size)] = middle
    m_ref[pl.ds(0, size), pl.ds(size, size)] = -times(t_ref[0], times(g_ref[0], t_ref[1]))
    far = times(g_ref[1], t_ref[2]) + times(g_ref[0], middle)
    m_ref[pl.ds(0, size), pl.ds(2 * size, size)] = -times(t_ref[0], far)


def mix(tri_factors, gram):
    size = 3 * tri_factors.shape[1]
    return pl.pallas_call(
        mix_kernel,
        in_specs=[NEAR, NEAR],
        out_specs=NEAR,
        out_shape=jax.ShapeDtypeStruct((size, size), jnp.float32),
        compiler_params=LIMIT,
    )(tri_factors, gram)


def columns_kernel(e_ref, o_ref, buf, in_sems, out_sems):
    blocks, depth, width = buf.shape
    arrivals = [
        pltpu.make_async_copy(e_ref.at[:, pl.ds(k * width, width)], buf.at[k], in_sems.at[k]) for k in range(blocks)
    ]
    leaves = [
        pltpu.make_async_copy(buf.at[k], o_ref.at[pl.ds(k * depth, depth)], out_sems.at[k]) for k in range(blocks)
    ]
    for copy in arrivals:
        copy.start()
    for arrival, leave in zip(arrivals, leaves):
        arrival.wait()
        leave.start()
    for leave in leaves:
        leave.wait()


def columns_apart(eigvecs, blocks):
    depth, width = eigvecs.shape[0], eigvecs.shape[1] // blocks
    return pl.pallas_call(
        columns_kernel,
        in_specs=[pl.BlockSpec(memory_space=pltpu.HBM)],
        out_specs=pl.BlockSpec(memory_space=pltpu.HBM),
        out_shape=jax.ShapeDtypeStruct((blocks * depth, width), jnp.float32),
        scratch_shapes=[
            pltpu.VMEM((blocks, depth, width), jnp.float32),
            pltpu.SemaphoreType.DMA((blocks,)),
            pltpu.SemaphoreType.DMA((blocks,)),
        ],
        compiler_params=LIMIT,
        cost_estimate=pl.CostEstimate(flops=0, bytes_accessed=8 * blocks * depth * width, transcendentals=0),
    )(eigvecs)


def scattered(values, axes):
    return lax.all_to_all(values, axes, split_axis=0, concat_axis=0, tiled=True)


def collected(parts, axes):
    groups = lax.axis_size(axes)
    total = jnp.sum(parts.reshape(groups, -1, parts.shape[1]), axis=0)
    spread = jnp.broadcast_to(total[None], (groups,) + total.shape).reshape(parts.shape)
    return lax.all_to_all(spread, axes, split_axis=0, concat_axis=0, tiled=True)


def turn(sign):
    size = lax.axis_size("x")
    pairs = []
    for x in range(size):
        for core in range(2):
            step = sign if core == 0 else -sign
            pairs.append((x * 2 + core, (x + step) % size * 2 + core))
    return pairs


def send(piece, sign):
    return lax.ppermute(piece, ("x", "core"), turn(sign))


def swap(piece, axis):
    return lax.ppermute(piece, axis, [(0, 1), (1, 0)])


def block_places():
    size = lax.axis_size("x")
    yhi, x, core = (lax.axis_index(name) for name in COL)
    places = []
    for c in (core, 1 - core):
        sign = 1 - 2 * c
        for y in (yhi, 1 - yhi):
            for step in (0, -1, 1, -2):
                places.append((y * size + lax.rem(x + sign * step + size, size)) * 2 + c)
    return jnp.stack(places).astype(jnp.int32)


def after(values, *done):
    tied = lax.optimization_barrier((*values, *done))
    return tied[: len(values)], tied[len(values) :]


def on_device(eigvecs, panels, tri_factors):
    count, block_size, depth = panels.shape
    start = (lax.axis_index(ROW) * lax.axis_size(COL) + lax.axis_index(COL)) * depth
    place = start + lax.broadcasted_iota(jnp.int32, (block_size, depth), 1)
    limit = lax.broadcasted_iota(jnp.int32, (block_size, depth), 0)
    shaped = []
    for j in range(count):
        gap = place - limit - (j + 1) * block_size
        shaped.append(jnp.where(gap < 0, 0.0, jnp.where(gap == 0, 1.0, panels[j])))
    places = block_places()

    wide = jnp.concatenate(shaped[:2], axis=0)
    slim = shaped[2]
    wide_there = swap(wide, "yhi")
    slim_near, slim_other = send(slim, 1), send(slim, -1)
    wide_near, wide_other = send(wide, 1), send(wide, -1)
    slim_far = send(slim_near, 1)
    early, (wide_there, wide_other) = after((slim, slim_near, slim_other), wide_there, wide_other)
    (wide_there,), (slim_far,) = after((wide_there,), slim_far)
    there_near, there_other = send(wide_there, 1), send(wide_there, -1)
    both = swap(jnp.concatenate(early[1:], axis=0), "yhi")
    slim_there, far_there = swap(early[0], "yhi"), swap(slim_far, "yhi")
    slim_held = [slim, slim_near, slim_other, slim_far]
    wide_held = [wide, wide_near, wide_other, send(wide_near, 1), wide_there, there_near, there_other]
    wide_held.append(send(there_near, 1))
    block = columns_apart(eigvecs, lax.axis_size(COL))
    (block,), held = after((block,), *wide_held[1:], *slim_held[1:], slim_there, both, far_there)
    wide_held[1:], slim_held[1:] = held[:7], held[7:10]
    slim_there, both, far_there = held[10:]
    slim_held += [slim_there, both[:block_size], both[block_size:], far_there]
    block = lax.all_to_all(block, COL, split_axis=0, concat_axis=0, tiled=True)
    pieces = list(zip(wide_held, slim_held))
    pieces += [tuple(swap(part, "core") for part in parts) for parts in pieces]

    gram, vectors = gram_of(pieces, block_size)
    size = lax.axis_size("z")
    for step in (1, 2):
        gram = gram + lax.ppermute(gram, "z", [(i, i ^ step) for i in range(size)])
    other = swap(gram, "ylo")
    parts = scattered(project(places, block, vectors), ROW)
    (other,), (parts,) = after((other,), parts)
    mixer = mix(tri_factors, gram + other)
    return apply(places, block, mixer, collected(parts, ROW), vectors)


def solution(mesh):
    fine = Mesh(mesh.devices.reshape(2, 4, 2, 4, 2), AXES)
    in_specs = (P(AXES, None), P(None, None, AXES), P())
    out_specs = P(ROW, COL)
    return jax.shard_map(on_device, mesh=fine, in_specs=in_specs, out_specs=out_specs, check_vma=False)
```
